128 devices in a mesh: clus: 32 (over y, x, core), rhs: 4 (over z).
Axes of the slice: x: 4, y: 4, z: 4, core: 2. Of those that a mesh axis runs over, the one named last changes fastest.
Arguments:
- sources: bfloat16 [128, 131072], P(None, 'clus'), may hold values from -6 to 6
- leaf_basis: bfloat16 [1024, 128, 64], P('clus'), may hold values from -0.5 to 0.5
- transfer: bfloat16 [1024, 64, 64], P('clus'), may hold values from -0.375 to 0.375
- far_leaf: int32 [1024, 8], P('clus'), may hold values from 0 to 1023
- leaf_coupling: bfloat16 [1024, 8, 64, 64], P('clus'), may hold values from -0.25 to 0.25
- far_par: int32 [256, 8], P('clus'), may hold values from 0 to 255
- par_coupling: bfloat16 [256, 8, 64, 64], P('clus'), may hold values from -0.25 to 0.25
- near_list: int32 [1024, 8], P('clus', 'rhs'), may hold values from 0 to 1023, as said below
- near_count: int32 [1024], P('clus'), may hold values from 3 to 8, as said below
- near_block: bfloat16 [1024, 8, 128, 128], P('clus', 'rhs'), may hold values from -0.25 to 0.25
Outputs:
- potential: bfloat16 [128, 131072], P('rhs', 'clus')
The draws below stay inside these ranges and needn't reach their ends.
Inputs may be any that keep to these rules, and one draw needn't show every extreme that they name: `near_list`: slot 0 of leaf t is t itself; every entry of leaf t names a leaf held by the same index of clus as t or by one of the two beside it (leaves are split in order, 32 to an index). Slot 1 names a leaf of the index before and slot 2 one of the index after, where those exist. `near_count`: slots at or past the count are not used; some leaf uses all 8; the count varies strongly between indices of clus.
All inputs are finite; a program needn't handle non-finite values.
Results may differ from the reference program's by a relative error of at most 0.0046.
Values may be sent and summed in bfloat16 or wider, within the bound.
No kernel may reach another device: no remote copies, remote signals or barrier semaphores. Data moves between devices by JAX's collectives and lax.ppermute only.
A program may use at most 128 MiB of HBM per device.

```python
import jax
import jax.numpy as jnp

LEAF = 128
K = 64
R = 128
LEAF_DEV = 32
NEAR = 8
FARL = 8
FARP = 8
LEAVES = 1024
PARENTS = 256
N = 131072


def draw_near_list(key, part):
    key = jax.random.fold_in(key, 11)
    key_prev, key_next, key_other = jax.random.split(key, 3)
    leaf_ids = jnp.arange(LEAVES, dtype=jnp.int32)
    devices = LEAVES // LEAF_DEV
    device = leaf_ids // LEAF_DEV
    own_base = device * LEAF_DEV
    lowest = jnp.maximum(device - 1, 0) * LEAF_DEV
    highest = (jnp.minimum(device + 1, devices - 1) + 1) * LEAF_DEV
    prev_base = jnp.where(device > 0, own_base - LEAF_DEV, own_base)
    next_base = jnp.where(device < devices - 1, own_base + LEAF_DEV, own_base)
    prev_pick = prev_base + jax.random.randint(key_prev, (LEAVES,), 0, LEAF_DEV)
    next_pick = next_base + jax.random.randint(key_next, (LEAVES,), 0, LEAF_DEV)
    window = highest - lowest
    others = lowest[:, None] + jax.random.randint(key_other, (LEAVES, NEAR - 3), 0, 1 << 20) % window[:, None]
    joined = jnp.concatenate([leaf_ids[:, None], prev_pick[:, None], next_pick[:, None], others], axis=1)
    return joined.astype(jnp.int32)


def draw_near_count(key, part):
    key = jax.random.fold_in(key, 23)
    key_level, key_extra = jax.random.split(key, 2)
    devices = LEAVES // LEAF_DEV
    level = jax.random.randint(key_level, (devices,), 0, NEAR - 2)
    extra = jax.random.randint(key_extra, (LEAVES,), 0, 1 << 20) % (jnp.repeat(level, LEAF_DEV) + 1)
    counts = 3 + extra
    counts = counts.at[0].set(NEAR)
    return counts.astype(jnp.int32)


def touch_ends(result, rng, smallest, high):
    spot = [jax.random.randint(jax.random.fold_in(rng, axis), (), 0, length) for axis, length in enumerate(result.shape)]
    main_axis = result.shape.index(max(result.shape))
    neighbour = spot[:main_axis] + [(spot[main_axis] + 1) % result.shape[main_axis]] + spot[main_axis + 1:]
    return result.at[tuple(spot)].set(smallest).at[tuple(neighbour)].set(high)


def steps_of(key, shape, pieces, smallest, top_value):
    loudness, own = 1.0, jax.random.fold_in(key, 6)
    for position, parts in pieces:
        draws = jnp.exp(jax.random.uniform(jax.random.fold_in(own, position), (parts,), jnp.float32, smallest / len(pieces), top_value / len(pieces)))
        loudness = loudness * jnp.repeat(draws, shape[position] // parts).reshape([-1 if axis == position else 1 for axis in range(len(shape))])
    return loudness


def bell_draw(key, dims, scale, limit, shards=(), held_as=jnp.bfloat16):
    factor_of = steps_of(key, dims, shards, -0.22, 0.18) if shards else 1.0
    drawn = jax.random.normal(key, dims, jnp.float32) * scale * factor_of
    return jnp.minimum(jnp.maximum(drawn, -limit), limit).astype(held_as)


def setup_inputs(seed: int = 0) -> dict:
    splits = jax.random.split(jax.random.key(seed), 11)
    sources = bell_draw(splits[0], (R, N), 1.0, 6.0, ((1, 32),))
    leaf_basis = bell_draw(splits[1], (LEAVES, LEAF, K), LEAF ** -0.5, 0.5, ((0, 32),))
    transfer = bell_draw(splits[2], (LEAVES, K, K), (4 * K) ** -0.5, 0.375, ((0, 32),))
    far_leaf = touch_ends(jax.random.randint(splits[3], (LEAVES, FARL), 0, LEAVES), jax.random.fold_in(splits[3], 1), 0, LEAVES - 1).astype(jnp.int32)
    leaf_coupling = bell_draw(splits[4], (LEAVES, FARL, K, K), (FARL * K) ** -0.5, 0.25, ((0, 32),))
    far_par = touch_ends(jax.random.randint(splits[5], (PARENTS, FARP), 0, PARENTS), jax.random.fold_in(splits[5], 1), 0, PARENTS - 1).astype(jnp.int32)
    par_coupling = bell_draw(splits[6], (PARENTS, FARP, K, K), (FARP * K) ** -0.5, 0.25, ((0, 32),))
    near_list = draw_near_list(jax.random.fold_in(splits[10], 71), 0)
    near_count = draw_near_count(jax.random.fold_in(splits[10], 71), 0)
    near_block = bell_draw(splits[9], (LEAVES, NEAR, LEAF, LEAF), (4 * LEAF) ** -0.5, 0.25, ((0, 32), (1, 4)))
    return dict(sources=sources, leaf_basis=leaf_basis, transfer=transfer, far_leaf=far_leaf, leaf_coupling=leaf_coupling, far_par=far_par, par_coupling=par_coupling, near_list=near_list, near_count=near_count, near_block=near_block)


def reference(sources, leaf_basis, transfer, far_leaf, leaf_coupling, far_par, par_coupling, near_list, near_count, near_block):
    blocks = sources.reshape(R, LEAVES, LEAF)
    leaf_coef = jnp.einsum('rlp,lpk->rlk', blocks.astype(jnp.float32), leaf_basis.astype(jnp.float32)).astype(jnp.bfloat16)
    lifted = jnp.einsum('rlj,ljk->rlk', leaf_coef.astype(jnp.float32), transfer.astype(jnp.float32))
    par_coef = lifted.reshape(R, PARENTS, 4, K).sum(axis=2).astype(jnp.bfloat16)
    leaf_source = jnp.take(leaf_coef, far_leaf, axis=1)
    leaf_field = jnp.einsum('tjab,rtjb->rta', leaf_coupling.astype(jnp.float32), leaf_source.astype(jnp.float32))
    par_source = jnp.take(par_coef, far_par, axis=1)
    par_field = jnp.einsum('qjab,rqjb->rqa', par_coupling.astype(jnp.float32), par_source.astype(jnp.float32)).astype(jnp.bfloat16)
    spread = jnp.repeat(par_field, 4, axis=1)
    downward = (leaf_field + jnp.einsum('ljk,rlk->rlj', transfer.astype(jnp.float32), spread.astype(jnp.float32))).astype(jnp.bfloat16)
    far_out = jnp.einsum('lpk,rlk->rlp', leaf_basis.astype(jnp.float32), downward.astype(jnp.float32))
    active = (jnp.arange(NEAR, dtype=jnp.int32)[None, :] < near_count[:, None]).astype(jnp.float32)
    near_source = jnp.take(blocks, near_list, axis=1).astype(jnp.float32) * active[None, :, :, None]
    near_out = jnp.einsum('tjpq,rtjq->rtp', near_block.astype(jnp.float32), near_source)
    return (far_out + near_out).reshape(R, N).astype(jnp.bfloat16)
```

```python
import jax
import jax.numpy as jnp
from jax import lax
from jax.experimental import pallas as pl
from jax.experimental.pallas import tpu as pltpu
from jax.sharding import PartitionSpec as P

BF16 = jnp.bfloat16
F32 = jnp.float32
LEAVES = 32
PARENTS = 8
ROWS = 640
SIDE = 4
STEP_PARENTS = 2
NT = (((1,), (1,)), ((), ()))


def dot_nt(a, b):
    return lax.dot_general(a, b, NT, preferred_element_type=F32)


def side_by_side(a, b):
    return jnp.concatenate([a, b], axis=1)


def diagonal(a, b):
    zeros = jnp.zeros_like(a)
    return jnp.concatenate([side_by_side(a, zeros), side_by_side(zeros, b)], axis=0)


def coef_kernel(meta, sources, basis, transfer, out):
    pairs = []
    for m in range(LEAVES // 2):
        weights = diagonal(basis[2 * m], basis[2 * m + 1])
        pair = dot_nt(sources[:, 256 * m : 256 * (m + 1)], weights).astype(BF16)
        out[32 * m : 32 * (m + 1), :] = pair
        pairs.append(pair)
    for n in range(PARENTS // 2):
        halves = []
        for q in (2 * n, 2 * n + 1):
            children = side_by_side(pairs[2 * q], pairs[2 * q + 1])
            weights = transfer[4 * q : 4 * q + 4].reshape(256, 64)
            halves.append(jnp.dot(children, weights, preferred_element_type=F32))
        out[512 + 32 * n : 512 + 32 * (n + 1), :] = side_by_side(*halves).astype(BF16)


def coefficients(meta, sources, basis, transfer):
    return pl.pallas_call(
        coef_kernel,
        out_shape=jax.ShapeDtypeStruct((ROWS, 128), BF16),
        grid_spec=pltpu.PrefetchScalarGridSpec(
            num_scalar_prefetch=1,
            grid=(1,),
            in_specs=[
                pl.BlockSpec((32, 4096), lambda i, meta: (meta[0], 0)),
                pl.BlockSpec((LEAVES, 64, 128), lambda i, meta: (0, 0, 0)),
                pl.BlockSpec((LEAVES, 64, 64), lambda i, meta: (0, 0, 0)),
            ],
            out_specs=pl.BlockSpec((ROWS, 128), lambda i, meta: (0, 0)),
        ),
        compiler_params=pltpu.CompilerParams(vmem_limit_bytes=32 << 20),
    )(meta, sources, basis, transfer)


def near_kernel(meta, near_list, near_count, own, before, after, near_block, *rest):
    outs, window, sems = rest[:4], rest[4], rest[5]
    copies = [
        pltpu.make_async_copy(part, window.at[:, pl.ds(4096 * k, 4096)], sems.at[k])
        for k, part in enumerate((before, own, after))
    ]
    for copy in copies:
        copy.start()
    for copy in copies:
        copy.wait()
    z = meta[0]
    first = (meta[1] - 1) * LEAVES

    def body(t, carry):
        parts = []
        for i in range(2):
            place = jnp.clip(near_list[i, t] - first, 0, 3 * LEAVES - 1)
            columns = pl.ds(pl.multiple_of(place * 128, 128), 128)
            active = z * 2 + i < near_count[t]
            rows = [
                window[pl.ds(pl.multiple_of(((z + d) % 4) * 32, 32), 32), columns]
                for d in range(4)
            ]
            block = jnp.concatenate(rows, axis=0)
            parts.append(lax.select(active, block, jnp.zeros_like(block)))
        weights = side_by_side(near_block[t, 0], near_block[t, 1])
        result = dot_nt(side_by_side(*parts), weights).astype(BF16)
        here = pl.ds(pl.multiple_of(t * 128, 128), 128)
        for d in range(4):
            outs[d][:, here] = result[32 * d : 32 * (d + 1)]
        return carry

    lax.fori_loop(0, LEAVES, body, 0, unroll=4)


def near_partials(meta, near_list, near_count, own, before, after, near_block):
    smem = pl.BlockSpec(memory_space=pltpu.SMEM)
    anywhere = pl.BlockSpec(memory_space=pl.ANY)
    return pl.pallas_call(
        near_kernel,
        out_shape=[jax.ShapeDtypeStruct((32, 4096), BF16)] * 4,
        in_specs=[smem] * 3 + [anywhere] * 3 + [pl.BlockSpec(memory_space=pltpu.VMEM)],
        out_specs=[pl.BlockSpec(memory_space=pltpu.VMEM)] * 4,
        scratch_shapes=[
            pltpu.VMEM((128, 3 * 4096), BF16),
            pltpu.SemaphoreType.DMA((3,)),
        ],
        compiler_params=pltpu.CompilerParams(vmem_limit_bytes=32 << 20),
    )(meta, near_list, near_count, own, before, after, near_block)


def chunk_places(y, x, alongx):
    def chip(first, second):
        dy, dx = (second, first) if alongx else (first, second)
        return ((y + dy + SIDE) % SIDE) * SIDE + (x + dx + SIDE) % SIDE

    order = (0, -1, 1, 2)
    own = [chip(s, 0) for s in order]
    sides = [chip(s, d) for d in (-1, 1) for s in order]
    far = [chip(s, 2) for s in order]
    return own, sides, far


def far_kernel(meta, far_leaf, far_par, *rest):
    (own, sides_b, sides_a, far_b, far_a, own2, sides2, far2) = rest[:8]
    coupling, par_coupling, transfer, basis, near0, near1, near2, near3, out, held, sems = rest[8:]
    step = pl.program_id(0)

    def copies(y, x, core):
        mine = chunk_places(y, x, core == 0)
        other = chunk_places(y, x, core == 1)
        pieces = []
        for k in range(4):
            pieces.append((own, k, mine[0][k], core))
            pieces.append((sides_b, k, mine[1][k], core))
            pieces.append((sides_a, k, mine[1][4 + k], core))
            pieces.append((far_b if k < 2 else far_a, k % 2, mine[2][k], core))
            pieces.append((own2, k, other[0][k], 1 - core))
            pieces.append((sides2, k, other[1][k], 1 - core))
            pieces.append((sides2, 4 + k, other[1][4 + k], 1 - core))
            pieces.append((far2, k, other[2][k], 1 - core))
        return [
            pltpu.make_async_copy(
                ref.at[pl.ds(ROWS * k, ROWS)], held.at[chip * 2 + c], sems.at[n]
            )
            for n, (ref, k, chip, c) in enumerate(pieces)
        ]

    @pl.when(step == 0)
    def _():
        y, x, core = meta[2], meta[3], meta[4]
        for which in range(2):

            @pl.when(core == which)
            def _():
                started = copies(y, x, which)
                for copy in started:
                    copy.start()
                for copy in started:
                    copy.wait()

    lane = lax.broadcasted_iota(jnp.int32, (1, 128), 1)
    low = (lane < 64).astype(F32).astype(BF16)
    high = (lane >= 64).astype(F32).astype(BF16)

    def leaf_pair(index):
        rows = pl.ds(pl.multiple_of((index % 32) // 2 * 32, 32), 32)
        return held[index // 32, rows, :] * lax.select(index % 2 == 0, low, high)

    def par_pair(index):
        rows = pl.ds(pl.multiple_of(512 + (index % 8) // 2 * 32, 32), 32)
        return held[index // 8, rows, :] * lax.select(index % 2 == 0, low, high)

    def couple(pick, indices, blocks):
        total = None
        for i in range(0, 8, 2):
            terms = side_by_side(pick(indices[i]), pick(indices[i + 1]))
            weights = jnp.concatenate(
                [blocks(i), blocks(i), blocks(i + 1), blocks(i + 1)], axis=1
            )
            term = dot_nt(terms, weights)
            total = term if total is None else total + term
        return total

    for p in range(STEP_PARENTS):
        q = step * STEP_PARENTS + p
        field = couple(
            par_pair, [far_par[q, i] for i in range(8)], lambda i: par_coupling[p, i]
        ).astype(BF16)
        spread = dot_nt(field, transfer[4 * p : 4 * p + 4].reshape(256, 64))
        for m in range(2):
            downs = []
            for c in (2 * m, 2 * m + 1):
                leaf = 4 * p + c
                local = couple(
                    leaf_pair,
                    [far_leaf[i, 4 * q + c] for i in range(8)],
                    lambda i: coupling[leaf, i],
                )
                downs.append(local + spread[:, 64 * c : 64 * (c + 1)])
            down = side_by_side(*downs).astype(BF16)
            leaf = 4 * p + 2 * m
            result = jnp.dot(
                down, diagonal(basis[leaf], basis[leaf + 1]), preferred_element_type=F32
            )
            here = slice(128 * leaf, 128 * (leaf + 2))
            near = near0[:, here].astype(F32) + near1[:, here].astype(F32)
            near += near2[:, here].astype(F32) + near3[:, here].astype(F32)
            out[:, here] = (result + near).astype(BF16)


def far_and_sum(meta, far_leaf, far_par, gathered, coupling, par_coupling, transfer, basis, nears):
    smem = pl.BlockSpec(memory_space=pltpu.SMEM)
    anywhere = pl.BlockSpec(memory_space=pl.ANY)
    leaves = 4 * STEP_PARENTS
    part = pl.BlockSpec((32, 128 * leaves), lambda i: (0, i))
    return pl.pallas_call(
        far_kernel,
        out_shape=jax.ShapeDtypeStruct((32, 4096), BF16),
        grid=(PARENTS // STEP_PARENTS,),
        in_specs=[smem] * 3
        + [anywhere] * 8
        + [
            pl.BlockSpec((leaves, 8, 64, 64), lambda i: (i, 0, 0, 0)),
            pl.BlockSpec((STEP_PARENTS, 8, 64, 64), lambda i: (i, 0, 0, 0)),
            pl.BlockSpec((leaves, 64, 64), lambda i: (i, 0, 0)),
            pl.BlockSpec((leaves, 64, 128), lambda i: (i, 0, 0)),
        ]
        + [part] * 4,
        out_specs=part,
        scratch_shapes=[
            pltpu.VMEM((32, ROWS, 128), BF16),
            pltpu.SemaphoreType.DMA((32,)),
        ],
        compiler_params=pltpu.CompilerParams(vmem_limit_bytes=40 << 20),
    )(meta, far_leaf, far_par, *gathered, coupling, par_coupling, transfer, basis, *nears)


def place(y, x, core):
    return (y % SIDE) * 8 + (x % SIDE) * 2 + core


def around(distance, first):
    pairs = []
    for y in range(SIDE):
        for x in range(SIDE):
            for core in range(2):
                alongx = (core == 0) == first
                to = place(y, x + distance, core) if alongx else place(y + distance, x, core)
                pairs.append((place(y, x, core), to))
    return pairs


SWAP = [(i, i ^ 1) for i in range(32)]


def gather(chunk):
    def send(value, pairs):
        return lax.ppermute(value, "clus", pairs)

    across = send(chunk, around(2, True))
    before = send(chunk, around(1, True))
    after = send(chunk, around(-1, True))
    own = jnp.concatenate([chunk, before, after, across], axis=0)
    half = own.shape[0] // 2
    side_b = send(own, around(1, False))
    side_a = send(own, around(-1, False))
    own2 = send(own, SWAP)
    far_b = send(side_b[:half], around(1, False))
    far_a = send(side_a[half:], around(-1, False))
    sides2 = send(jnp.concatenate([side_b, side_a], axis=0), SWAP)
    far2 = send(jnp.concatenate([far_b, far_a], axis=0), SWAP)
    return own, side_b, side_a, far_b, far_a, own2, sides2, far2


def per_device(
    sources,
    leaf_basis,
    transfer,
    far_leaf,
    leaf_coupling,
    far_par,
    par_coupling,
    near_list,
    near_count,
    near_block,
):
    clus, rhs = lax.axis_index("clus"), lax.axis_index("rhs")
    meta = jnp.stack([rhs, clus, clus // 8, (clus // 2) % 4, clus % 2]).astype(jnp.int32)
    basis = jnp.swapaxes(leaf_basis, 1, 2)
    before = lax.ppermute(sources, "clus", [(i, (i + 1) % 32) for i in range(32)])
    after = lax.ppermute(sources, "clus", [((i + 1) % 32, i) for i in range(32)])
    chunk = coefficients(meta, sources, basis, transfer)
    gathered = gather(chunk)
    partials = near_partials(
        meta, near_list.T, near_count, sources, before, after, near_block
    )
    nears = [partials[0]]
    for d in (1, 2, 3):
        nears.append(lax.ppermute(partials[d], "rhs", [(j, (j + d) % 4) for j in range(4)]))
    return far_and_sum(
        meta, far_leaf.T, far_par, gathered, leaf_coupling, par_coupling, transfer, basis, nears
    )


def solution(mesh):
    in_specs = (
        P(None, "clus"),
        P("clus", None, None),
        P("clus", None, None),
        P("clus", None),
        P("clus", None, None, None),
        P("clus", None),
        P("clus", None, None, None),
        P("clus", "rhs"),
        P("clus"),
        P("clus", "rhs", None, None),
    )
    return jax.shard_map(
        per_device, mesh=mesh, in_specs=in_specs, out_specs=P("rhs", "clus"), check_vma=False
    )
```

```python
import jax
import jax.numpy as jnp
from jax import lax
from jax.experimental import pallas as pl
from jax.experimental.pallas import tpu as pltpu
from jax.sharding import PartitionSpec as P

BF16 = jnp.bfloat16
F32 = jnp.float32
LEAVES = 32
PARENTS = 8
ROWS = 640
SIDE = 4
NT = (((1,), (1,)), ((), ()))


def dot_nt(a, b):
    return lax.dot_general(a, b, NT, preferred_element_type=F32)


def side_by_side(a, b):
    return jnp.concatenate([a, b], axis=1)


def diagonal(a, b):
    zeros = jnp.zeros_like(a)
    return jnp.concatenate([side_by_side(a, zeros), side_by_side(zeros, b)], axis=0)


def coef_kernel(meta, sources, basis, transfer, out, rows, basis_here, transfer_here, sems):
    z = meta[0]
    copies = [
        pltpu.make_async_copy(sources.at[pl.ds(pl.multiple_of(z * 32, 32), 32), :], rows, sems.at[0]),
        pltpu.make_async_copy(basis, basis_here, sems.at[1]),
        pltpu.make_async_copy(transfer, transfer_here, sems.at[2]),
    ]
    for copy in copies:
        copy.start()
    copies[0].wait()
    copies[1].wait()
    pairs = []
    for m in range(LEAVES // 2):
        weights = diagonal(basis_here[2 * m], basis_here[2 * m + 1])
        pair = dot_nt(rows[:, 256 * m : 256 * (m + 1)], weights).astype(BF16)
        out[32 * m : 32 * (m + 1), :] = pair
        pairs.append(pair)
    copies[2].wait()
    for n in range(PARENTS // 2):
        halves = []
        for q in (2 * n, 2 * n + 1):
            children = side_by_side(pairs[2 * q], pairs[2 * q + 1])
            weights = transfer_here[4 * q : 4 * q + 4].reshape(256, 64)
            halves.append(jnp.dot(children, weights, preferred_element_type=F32))
        out[512 + 32 * n : 512 + 32 * (n + 1), :] = side_by_side(*halves).astype(BF16)


def coefficients(meta, sources, basis, transfer):
    hbm = pl.BlockSpec(memory_space=pltpu.HBM)
    return pl.pallas_call(
        coef_kernel,
        out_shape=jax.ShapeDtypeStruct((ROWS, 128), BF16),
        in_specs=[pl.BlockSpec(memory_space=pltpu.SMEM)] + [hbm] * 3,
        out_specs=pl.BlockSpec(memory_space=pltpu.VMEM),
        scratch_shapes=[
            pltpu.VMEM((32, 4096), BF16),
            pltpu.VMEM((LEAVES, 64, 128), BF16),
            pltpu.VMEM((LEAVES, 64, 64), BF16),
            pltpu.SemaphoreType.DMA((3,)),
        ],
        compiler_params=pltpu.CompilerParams(vmem_limit_bytes=8 << 20),
    )(meta, sources, basis, transfer)


def near_kernel(meta, near_list, near_count, own, before, after, near_block, *rest):
    keep, pass_on, give, window, sems = rest
    copies = [
        pltpu.make_async_copy(part, window.at[:, pl.ds(4096 * k, 4096)], sems.at[k])
        for k, part in enumerate((before, own, after))
    ]
    for copy in copies:
        copy.start()
    for copy in copies:
        copy.wait()
    z, core = meta[0], meta[1] & 1
    first = (meta[1] - 1) * LEAVES
    owners = (z, z ^ jnp.where(core == 0, 3, 1), z ^ jnp.where(core == 0, 1, 3), z ^ 2)

    def body(t, carry):
        parts = []
        for i in range(2):
            place = jnp.clip(near_list[i, t] - first, 0, 3 * LEAVES - 1)
            columns = pl.ds(pl.multiple_of(place * 128, 128), 128)
            active = z * 2 + i < near_count[t]
            rows = [
                window[pl.ds(pl.multiple_of(owner * 32, 32), 32), columns] for owner in owners
            ]
            block = jnp.concatenate(rows, axis=0)
            parts.append(lax.select(active, block, jnp.zeros_like(block)))
        weights = side_by_side(near_block[t, 0], near_block[t, 1])
        result = dot_nt(side_by_side(*parts), weights).astype(BF16)
        here = pl.ds(pl.multiple_of(t * 128, 128), 128)
        keep[:, here] = result[:32]
        pass_on[:, here] = result[32:64]
        give[:, here] = result[64:]
        return carry

    lax.fori_loop(0, LEAVES, body, 0, unroll=4)


def near_partials(meta, near_list, near_count, own, before, after, near_block):
    smem = pl.BlockSpec(memory_space=pltpu.SMEM)
    anywhere = pl.BlockSpec(memory_space=pl.ANY)
    return pl.pallas_call(
        near_kernel,
        out_shape=[jax.ShapeDtypeStruct((n, 4096), BF16) for n in (32, 32, 64)],
        in_specs=[smem] * 3 + [anywhere] * 3 + [pl.BlockSpec(memory_space=pltpu.VMEM)],
        out_specs=[pl.BlockSpec(memory_space=pltpu.VMEM)] * 3,
        scratch_shapes=[
            pltpu.VMEM((128, 3 * 4096), BF16),
            pltpu.SemaphoreType.DMA((3,)),
        ],
        compiler_params=pltpu.CompilerParams(vmem_limit_bytes=12 << 20),
    )(meta, near_list, near_count, own, before, after, near_block)


def far_kernel(leaf_codes, par_codes, held, coupling, par_coupling, transfer, basis, *rest):
    nears, out = rest[:3], rest[3]
    lane = lax.broadcasted_iota(jnp.int32, (1, 128), 1)
    low = (lane < 64).astype(F32).astype(BF16)
    high = (lane >= 64).astype(F32).astype(BF16)

    def turned(code, wanted):
        pair = held[pl.ds(pl.multiple_of(code & ~31, 32), 32), :]
        swapped = side_by_side(pair[:, 64:], pair[:, :64])
        return lax.select((code & 1) == wanted, pair, swapped)

    def couple(codes, blocks):
        terms, weights = [], []
        for i in range(0, 8, 2):
            terms.append(turned(codes[i], 0) * low + turned(codes[i + 1], 1) * high)
            weights.append(side_by_side(blocks(i), blocks(i + 1)))
        return dot_nt(jnp.concatenate(terms, axis=1), jnp.concatenate(weights, axis=1))

    def body(q, carry):
        field = couple([par_codes[q, i] for i in range(8)], lambda i: par_coupling[q, i])
        spread = dot_nt(field.astype(BF16), transfer[pl.ds(4 * q, 4)].reshape(256, 64))
        for m in range(2):
            downs = []
            for c in (2 * m, 2 * m + 1):
                leaf = 4 * q + c
                codes = [leaf_codes[i, leaf] for i in range(8)]
                local = couple(codes, lambda i: coupling[leaf, i])
                downs.append(local + spread[:, 64 * c : 64 * (c + 1)])
            down = side_by_side(*downs).astype(BF16)
            leaf = 4 * q + 2 * m
            weights = diagonal(basis[leaf], basis[leaf + 1])
            result = jnp.dot(down, weights, preferred_element_type=F32)
            here = pl.ds(pl.multiple_of(128 * leaf, 256), 256)
            for near in nears:
                result += near[:32, here].astype(F32)
            out[:, here] = result.astype(BF16)
        return carry

    lax.fori_loop(0, PARENTS, body, 0, unroll=True)


def far_and_sum(leaf_codes, par_codes, held, coupling, par_coupling, transfer, basis, nears):
    smem = pl.BlockSpec(memory_space=pltpu.SMEM)
    vmem = pl.BlockSpec(memory_space=pltpu.VMEM)
    return pl.pallas_call(
        far_kernel,
        out_shape=jax.ShapeDtypeStruct((32, 4096), BF16),
        in_specs=[smem] * 2 + [vmem] * 8,
        out_specs=vmem,
        compiler_params=pltpu.CompilerParams(vmem_limit_bytes=18 << 20),
    )(leaf_codes, par_codes, held, coupling, par_coupling, transfer, basis, *nears)


def place(y, x, core):
    return (y % SIDE) * 8 + (x % SIDE) * 2 + core


def around(distance, first):
    pairs = []
    for y in range(SIDE):
        for x in range(SIDE):
            for core in range(2):
                alongx = (core == 0) == first
                to = place(y, x + distance, core) if alongx else place(y + distance, x, core)
                pairs.append((place(y, x, core), to))
    return pairs


def partners(first):
    return [
        (c * 4 + z, c * 4 + (z ^ (1 if (c % 2 == 0) == first else 3)))
        for c in range(32)
        for z in range(4)
    ]


SWAP = [(i, i ^ 1) for i in range(32)]


def send(value, pairs):
    return lax.ppermute(value, "clus", pairs)


def joined(*parts):
    return jnp.concatenate(parts, axis=0)


def codes_of(index, shift, first_row, y, x, core):
    source = index >> shift
    sy, sx, score = source >> 3, (source >> 1) & 3, source & 1
    dy, dx = (sy - y) & 3, (sx - x) & 3
    inner = jnp.where(score == 0, dx, dy)
    outer = jnp.where(score == 0, dy, dx)

    def rank(distance):
        return (0x78 >> (2 * distance)) & 3

    chunk = jnp.where(score == core, 0, 16) + 4 * rank(outer) + rank(inner)
    pair = (index & ((1 << shift) - 1)) >> 1
    return (chunk * ROWS + first_row + pair * 32) | (index & 1)


def per_device(
    sources,
    leaf_basis,
    transfer,
    far_leaf,
    leaf_coupling,
    far_par,
    par_coupling,
    near_list,
    near_count,
    near_block,
):
    clus, rhs = lax.axis_index("clus"), lax.axis_index("rhs")
    y, x, core = clus >> 3, (clus >> 1) & 3, clus & 1
    meta = jnp.stack([rhs, clus]).astype(jnp.int32)
    leaf_codes = codes_of(far_leaf.T, 5, 0, y, x, core)
    par_codes = codes_of(far_par, 3, 512, y, x, core)
    basis = jnp.swapaxes(leaf_basis, 1, 2)
    halo_before = send(sources, [(i, (i + 1) % 32) for i in range(32)])
    halo_after = send(sources, [((i + 1) % 32, i) for i in range(32)])
    chunk = coefficients(meta, sources, basis, transfer)

    before = send(chunk, around(1, True))
    after = send(chunk, around(-1, True))
    across = send(chunk, around(2, True))
    before, after, across, halo_before, halo_after = lax.optimization_barrier(
        (before, after, across, halo_before, halo_after)
    )
    own = joined(chunk, before, after, across)
    side_b = send(own, around(1, False))
    side_a = send(own, around(-1, False))
    keep, pass_on, give = near_partials(
        meta, near_list.T, near_count, sources, halo_before, halo_after, near_block
    )
    taken = lax.ppermute(give, ("clus", "rhs"), partners(True))
    side_b, side_a, pass_on = lax.optimization_barrier((side_b, side_a, pass_on))
    half = own.shape[0] // 2
    far_b = send(side_b[:half], around(1, False))
    far_a = send(side_a[half:], around(-1, False))
    pass_on = (pass_on.astype(F32) + taken[32:].astype(F32)).astype(BF16)
    far_b, far_a, pass_on = lax.optimization_barrier((far_b, far_a, pass_on))
    nears = (keep, taken, lax.ppermute(pass_on, ("clus", "rhs"), partners(False)))
    sides, far = joined(side_b, side_a), joined(far_b, far_a)
    held = joined(own, sides, far, send(own, SWAP), send(sides, SWAP), send(far, SWAP))
    return far_and_sum(
        leaf_codes, par_codes, held, leaf_coupling, par_coupling, transfer, basis, nears
    )


def solution(mesh):
    in_specs = (
        P(None, "clus"),
        P("clus", None, None),
        P("clus", None, None),
        P("clus", None),
        P("clus", None, None, None),
        P("clus", None),
        P("clus", None, None, None),
        P("clus", "rhs"),
        P("clus"),
        P("clus", "rhs", None, None),
    )
    return jax.shard_map(
        per_device, mesh=mesh, in_specs=in_specs, out_specs=P("rhs", "clus"), check_vma=False
    )
```

```python
import jax
import jax.numpy as jnp
from jax import lax
from jax.experimental import pallas as pl
from jax.experimental.pallas import tpu as pltpu
from jax.sharding import PartitionSpec as P

BF16 = jnp.bfloat16
F32 = jnp.float32
LEAVES = 32
PARENTS = 8
ROWS = 640
SIDE = 4
NT = (((1,), (1,)), ((), ()))


def dot_nt(a, b):
    return lax.dot_general(a, b, NT, preferred_element_type=F32)


def side_by_side(a, b):
    return jnp.concatenate([a, b], axis=1)


def diagonal(a, b):
    zeros = jnp.zeros_like(a)
    return jnp.concatenate([side_by_side(a, zeros), side_by_side(zeros, b)], axis=0)


def codes_of(index, shift, first_row, y, x, core):
    source = index >> shift
    dy, dx = ((source >> 3) - y) & 3, ((source >> 1) - x) & 3
    along_x = (source & 1) == 0
    inner, outer = jnp.where(along_x, dx, dy), jnp.where(along_x, dy, dx)

    def rank(distance):
        return jnp.where(distance == 0, 0, jnp.where(distance == 3, 1, distance + 1))

    chunk = ((source ^ core) & 1) * 16 + 4 * rank(outer) + rank(inner)
    pair = (index & ((1 << shift) - 1)) >> 1
    return (chunk * ROWS + first_row + pair * 32) | (index & 1)


def coef_kernel(meta, *refs):
    sources, basis, transfer, far_leaf, far_par, near_list, near_count, near_block = refs[:8]
    out, leaf_codes, par_codes, near_codes, own, near_here = refs[8:14]
    rows, basis_here, transfer_here, leaf_here, par_here, list_here, count_here, sems = refs[14:]
    z, clus = meta[0], meta[1]
    mine = sources.at[pl.ds(pl.multiple_of(z * 32, 32), 32), :]
    moves = (
        (mine, rows),
        (basis, basis_here),
        (transfer, transfer_here),
        (far_leaf, leaf_here),
        (far_par, par_here),
        (near_list, list_here),
        (near_count, count_here),
        (sources, own),
        (near_block, near_here),
    )
    copies = [pltpu.make_async_copy(a, b, sems.at[n]) for n, (a, b) in enumerate(moves)]
    for copy in copies:
        copy.start()
    for copy in copies[:7]:
        copy.wait()
    y, x, core = clus >> 3, (clus >> 1) & 3, clus & 1
    leaf_codes[...] = codes_of(leaf_here[...], 5, 0, y, x, core)
    par_codes[...] = codes_of(par_here[...], 3, 512, y, x, core)
    slot = z * 2 + lax.broadcasted_iota(jnp.int32, (2, LEAVES), 0)
    place = jnp.clip(list_here[...] - (clus - 1) * LEAVES, 0, 3 * LEAVES - 1)
    near_codes[...] = jnp.where(slot < count_here[...], place, -1)
    pairs = []
    for m in range(LEAVES // 2):
        weights = diagonal(basis_here[2 * m], basis_here[2 * m + 1])
        pair = dot_nt(rows[:, 256 * m : 256 * (m + 1)], weights).astype(BF16)
        out[32 * m : 32 * (m + 1), :] = pair
        pairs.append(pair)
    for n in range(PARENTS // 2):
        halves = []
        for q in (2 * n, 2 * n + 1):
            children = side_by_side(pairs[2 * q], pairs[2 * q + 1])
            weights = transfer_here[4 * q : 4 * q + 4].reshape(256, 64)
            halves.append(jnp.dot(children, weights, preferred_element_type=F32))
        out[512 + 32 * n : 512 + 32 * (n + 1), :] = side_by_side(*halves).astype(BF16)
    for copy in copies[7:]:
        copy.wait()


def coefficients(meta, *arrays):
    hbm = pl.BlockSpec(memory_space=pltpu.HBM)
    vmem = pl.BlockSpec(memory_space=pltpu.VMEM)
    tables = [(8, LEAVES), (PARENTS, 8), (2, LEAVES)]
    return pl.pallas_call(
        coef_kernel,
        out_shape=[pltpu.VMEM((ROWS, 128), BF16)]
        + [jax.ShapeDtypeStruct(table, jnp.int32) for table in tables]
        + [pltpu.VMEM((128, 4096), BF16), pltpu.VMEM((LEAVES, 2, 128, 128), BF16)],
        in_specs=[pl.BlockSpec(memory_space=pltpu.SMEM)] + [hbm] * 8,
        out_specs=[vmem] * 6,
        scratch_shapes=[
            pltpu.VMEM((32, 4096), BF16),
            pltpu.VMEM((LEAVES, 64, 128), BF16),
            pltpu.VMEM((LEAVES, 64, 64), BF16),
            pltpu.VMEM(tables[0], jnp.int32),
            pltpu.VMEM(tables[1], jnp.int32),
            pltpu.VMEM(tables[2], jnp.int32),
            pltpu.VMEM((1, LEAVES), jnp.int32),
            pltpu.SemaphoreType.DMA((9,)),
        ],
        compiler_params=pltpu.CompilerParams(vmem_limit_bytes=8 << 20),
    )(meta, *(pltpu.with_memory_space_constraint(array, pltpu.HBM) for array in arrays))


def stack_kernel(*refs):
    out = refs[-1]
    for k, part in enumerate(refs[:-1]):
        out[ROWS * k : ROWS * (k + 1), :] = part[...]


def stacked(*parts):
    vmem = pl.BlockSpec(memory_space=pltpu.VMEM)
    return pl.pallas_call(
        stack_kernel,
        out_shape=pltpu.VMEM((ROWS * len(parts), 128), BF16),
        in_specs=[vmem] * len(parts),
        out_specs=vmem,
        compiler_params=pltpu.CompilerParams(vmem_limit_bytes=4 << 20),
    )(*(pltpu.with_memory_space_constraint(part, pltpu.VMEM) for part in parts))


def near_kernel(meta, near_codes, own, before, after, near_block, keep, pass_on, give):
    z, core = meta[0], meta[1] & 1
    owners = (z, z ^ jnp.where(core == 0, 3, 1), z ^ jnp.where(core == 0, 1, 3), z ^ 2)

    def body(t, carry):
        parts = []
        for i in range(2):
            code = near_codes[i, t]
            index = jnp.maximum(code, 0)
            columns = pl.ds(pl.multiple_of((index & 31) * 128, 128), 128)
            rows = []
            for owner in owners:
                here = pl.ds(pl.multiple_of(owner * 32, 32), 32)
                outer = lax.select(index < 32, before[here, columns], after[here, columns])
                inside = (index >> 5) == 1
                rows.append(lax.select(inside, own[here, columns], outer))
            block = jnp.concatenate(rows, axis=0)
            parts.append(lax.select(code >= 0, block, jnp.zeros_like(block)))
        weights = side_by_side(near_block[t, 0], near_block[t, 1])
        result = dot_nt(side_by_side(*parts), weights).astype(BF16)
        here = pl.ds(pl.multiple_of(t * 128, 128), 128)
        keep[:, here] = result[:32]
        pass_on[:, here] = result[32:64]
        give[:, here] = result[64:]
        return carry

    lax.fori_loop(0, LEAVES, body, 0, unroll=8)


def near_partials(meta, near_codes, own, before, after, near_block):
    smem = pl.BlockSpec(memory_space=pltpu.SMEM)
    vmem = pl.BlockSpec(memory_space=pltpu.VMEM)
    return pl.pallas_call(
        near_kernel,
        out_shape=[jax.ShapeDtypeStruct((n, 4096), BF16) for n in (32, 32, 64)],
        in_specs=[smem] * 2 + [vmem] * 4,
        out_specs=[vmem] * 3,
        compiler_params=pltpu.CompilerParams(vmem_limit_bytes=12 << 20),
    )(meta, near_codes, own, before, after, near_block)


def far_kernel(leaf_codes, par_codes, held, coupling, par_coupling, transfer, basis, *rest):
    nears, out = rest[:3], rest[3]
    lane = lax.broadcasted_iota(jnp.int32, (1, 128), 1)
    low = (lane < 64).astype(F32).astype(BF16)
    high = (lane >= 64).astype(F32).astype(BF16)

    def turned(code, wanted):
        pair = held[pl.ds(pl.multiple_of(code & ~31, 32), 32), :]
        swapped = side_by_side(pair[:, 64:], pair[:, :64])
        return lax.select((code & 1) == wanted, pair, swapped)

    def couple(codes, blocks):
        terms, weights = [], []
        for i in range(0, 8, 2):
            terms.append(turned(codes[i], 0) * low + turned(codes[i + 1], 1) * high)
            weights.append(side_by_side(blocks(i), blocks(i + 1)))
        return dot_nt(jnp.concatenate(terms, axis=1), jnp.concatenate(weights, axis=1))

    def body(q, carry):
        field = couple([par_codes[q, i] for i in range(8)], lambda i: par_coupling[q, i])
        spread = dot_nt(field.astype(BF16), transfer[pl.ds(4 * q, 4)].reshape(256, 64))
        for m in range(2):
            downs = []
            for c in (2 * m, 2 * m + 1):
                leaf = 4 * q + c
                codes = [leaf_codes[i, leaf] for i in range(8)]
                local = couple(codes, lambda i: coupling[leaf, i])
                downs.append(local + spread[:, 64 * c : 64 * (c + 1)])
            down = side_by_side(*downs).astype(BF16)
            leaf = 4 * q + 2 * m
            weights = diagonal(basis[leaf], basis[leaf + 1])
            result = jnp.dot(down, weights, preferred_element_type=F32)
            here = pl.ds(pl.multiple_of(128 * leaf, 256), 256)
            for near in nears:
                result += near[:32, here].astype(F32)
            out[:, here] = result.astype(BF16)
        return carry

    lax.fori_loop(0, PARENTS, body, 0, unroll=True)


def far_and_sum(leaf_codes, par_codes, held, coupling, par_coupling, transfer, basis, nears):
    smem = pl.BlockSpec(memory_space=pltpu.SMEM)
    vmem = pl.BlockSpec(memory_space=pltpu.VMEM)
    return pl.pallas_call(
        far_kernel,
        out_shape=jax.ShapeDtypeStruct((32, 4096), BF16),
        in_specs=[smem] * 2 + [vmem] * 8,
        out_specs=vmem,
        compiler_params=pltpu.CompilerParams(vmem_limit_bytes=18 << 20),
    )(leaf_codes, par_codes, held, coupling, par_coupling, transfer, basis, *nears)


def place(y, x, core):
    return (y % SIDE) * 8 + (x % SIDE) * 2 + core


def around(distance, first):
    pairs = []
    for y in range(SIDE):
        for x in range(SIDE):
            for core in range(2):
                alongx = (core == 0) == first
                to = place(y, x + distance, core) if alongx else place(y + distance, x, core)
                pairs.append((place(y, x, core), to))
    return pairs


def partners(first):
    return [
        (c * 4 + z, c * 4 + (z ^ (1 if (c % 2 == 0) == first else 3)))
        for c in range(32)
        for z in range(4)
    ]


SWAP = [(i, i ^ 1) for i in range(32)]


def send(value, pairs):
    return lax.ppermute(value, "clus", pairs)


def joined(*parts):
    return jnp.concatenate(parts, axis=0)


def per_device(
    sources,
    leaf_basis,
    transfer,
    far_leaf,
    leaf_coupling,
    far_par,
    par_coupling,
    near_list,
    near_count,
    near_block,
):
    clus, rhs = lax.axis_index("clus"), lax.axis_index("rhs")
    meta = jnp.stack([rhs, clus]).astype(jnp.int32)
    basis = jnp.swapaxes(leaf_basis, 1, 2)
    halo_before = send(sources, [(i, (i + 1) % 32) for i in range(32)])
    halo_after = send(sources, [((i + 1) % 32, i) for i in range(32)])
    chunk, leaf_codes, par_codes, near_codes, sources_here, near_here = coefficients(
        meta,
        sources,
        basis,
        transfer,
        far_leaf.T,
        far_par,
        near_list.T,
        near_count.reshape(1, -1),
        near_block,
    )

    across = send(chunk, around(2, True))
    before = send(chunk, around(1, True))
    after = send(chunk, around(-1, True))
    before, after, across, halo_before, halo_after = lax.optimization_barrier(
        (before, after, across, halo_before, halo_after)
    )
    own = stacked(chunk, before, after, across)
    side_b = send(own, around(1, False))
    side_a = send(own, around(-1, False))
    keep, pass_on, give = near_partials(
        meta, near_codes, sources_here, halo_before, halo_after, near_here
    )
    taken = lax.ppermute(give, ("clus", "rhs"), partners(True))
    side_b, side_a, pass_on = lax.optimization_barrier((side_b, side_a, pass_on))
    half = own.shape[0] // 2
    far_b = send(side_b[:half], around(1, False))
    far_a = send(side_a[half:], around(-1, False))
    pass_on = (pass_on.astype(F32) + taken[32:].astype(F32)).astype(BF16)
    passed = lax.ppermute(pass_on, ("clus", "rhs"), partners(False))
    far_b, far_a, passed = lax.optimization_barrier((far_b, far_a, passed))
    nears = (keep, taken, passed)
    sides, far = joined(side_b, side_a), joined(far_b, far_a)
    held = joined(own, sides, far, send(own, SWAP), send(sides, SWAP), send(far, SWAP))
    return far_and_sum(
        leaf_codes, par_codes, held, leaf_coupling, par_coupling, transfer, basis, nears
    )


def solution(mesh):
    in_specs = (
        P(None, "clus"),
        P("clus", None, None),
        P("clus", None, None),
        P("clus", None),
        P("clus", None, None, None),
        P("clus", None),
        P("clus", None, None, None),
        P("clus", "rhs"),
        P("clus"),
        P("clus", "rhs", None, None),
    )
    return jax.shard_map(
        per_device, mesh=mesh, in_specs=in_specs, out_specs=P("rhs", "clus"), check_vma=False
    )
```

```python
import jax
import jax.numpy as jnp
from jax import lax
from jax.experimental import pallas as pl
from jax.experimental.pallas import tpu as pltpu
from jax.sharding import PartitionSpec as P

BF16 = jnp.bfloat16
F32 = jnp.float32
LEAVES = 32
PARENTS = 8
ROWS = 640
SIDE = 4
COEF_US, STACK_US, NEAR_US, FAR_US, ADD_US = 3, 0, 3, 3, 10
NT = (((1,), (1,)), ((), ()))


def cost(us):
    return pl.CostEstimate(flops=us * 10**9, bytes_accessed=us * 35 * 10**5, transcendentals=0)


def dot_nt(a, b):
    return lax.dot_general(a, b, NT, preferred_element_type=F32)


def side_by_side(a, b):
    return jnp.concatenate([a, b], axis=1)


def diagonal(a, b):
    zeros = jnp.zeros_like(a)
    return jnp.concatenate([side_by_side(a, zeros), side_by_side(zeros, b)], axis=0)


def codes_of(index, shift, first_row, y, x, core):
    source = index >> shift
    dy, dx = ((source >> 3) - y) & 3, ((source >> 1) - x) & 3
    along_x = (source & 1) == 0
    inner, outer = jnp.where(along_x, dx, dy), jnp.where(along_x, dy, dx)

    def rank(distance):
        return jnp.where(distance == 0, 0, jnp.where(distance == 3, 1, distance + 1))

    chunk = ((source ^ core) & 1) * 16 + 4 * rank(outer) + rank(inner)
    pair = (index & ((1 << shift) - 1)) >> 1
    return (chunk * ROWS + first_row + pair * 32) | (index & 1)


def coef_kernel(meta, *refs):
    sources, basis, transfer, far_leaf, far_par, near_list, near_count, near_block = refs[:8]
    out, leaf_codes, par_codes, near_codes, own, near_here = refs[8:14]
    rows, basis_here, transfer_here, leaf_here, par_here, list_here, count_here, sems = refs[14:]
    z, clus = meta[0], meta[1]
    mine = sources.at[pl.ds(pl.multiple_of(z * 32, 32), 32), :]
    moves = (
        (mine, rows),
        (basis, basis_here),
        (transfer, transfer_here),
        (far_leaf, leaf_here),
        (far_par, par_here),
        (near_list, list_here),
        (near_count, count_here),
        (sources, own),
        (near_block, near_here),
    )
    copies = [pltpu.make_async_copy(a, b, sems.at[n]) for n, (a, b) in enumerate(moves)]
    for copy in copies:
        copy.start()
    for copy in copies[:7]:
        copy.wait()
    y, x, core = clus >> 3, (clus >> 1) & 3, clus & 1
    leaf_codes[...] = codes_of(leaf_here[...], 5, 0, y, x, core)
    par_codes[...] = codes_of(par_here[...], 3, 512, y, x, core)
    slot = z * 2 + lax.broadcasted_iota(jnp.int32, (2, LEAVES), 0)
    place = jnp.clip(list_here[...] - (clus - 1) * LEAVES, 0, 3 * LEAVES - 1)
    near_codes[...] = jnp.where(slot < count_here[...], place, -1)
    pairs = []
    for m in range(LEAVES // 2):
        weights = diagonal(basis_here[2 * m], basis_here[2 * m + 1])
        pair = dot_nt(rows[:, 256 * m : 256 * (m + 1)], weights).astype(BF16)
        out[32 * m : 32 * (m + 1), :] = pair
        pairs.append(pair)
    for n in range(PARENTS // 2):
        halves = []
        for q in (2 * n, 2 * n + 1):
            children = side_by_side(pairs[2 * q], pairs[2 * q + 1])
            weights = transfer_here[4 * q : 4 * q + 4].reshape(256, 64)
            halves.append(jnp.dot(children, weights, preferred_element_type=F32))
        out[512 + 32 * n : 512 + 32 * (n + 1), :] = side_by_side(*halves).astype(BF16)
    for copy in copies[7:]:
        copy.wait()


def coefficients(meta, *arrays):
    hbm = pl.BlockSpec(memory_space=pltpu.HBM)
    vmem = pl.BlockSpec(memory_space=pltpu.VMEM)
    tables = [(8, LEAVES), (PARENTS, 8), (2, LEAVES)]
    return pl.pallas_call(
        coef_kernel,
        out_shape=[pltpu.VMEM((ROWS, 128), BF16)]
        + [jax.ShapeDtypeStruct(table, jnp.int32) for table in tables]
        + [pltpu.VMEM((128, 4096), BF16), pltpu.VMEM((LEAVES, 2, 128, 128), BF16)],
        in_specs=[pl.BlockSpec(memory_space=pltpu.SMEM)] + [hbm] * 8,
        out_specs=[vmem] * 6,
        scratch_shapes=[
            pltpu.VMEM((32, 4096), BF16),
            pltpu.VMEM((LEAVES, 64, 128), BF16),
            pltpu.VMEM((LEAVES, 64, 64), BF16),
            pltpu.VMEM(tables[0], jnp.int32),
            pltpu.VMEM(tables[1], jnp.int32),
            pltpu.VMEM(tables[2], jnp.int32),
            pltpu.VMEM((1, LEAVES), jnp.int32),
            pltpu.SemaphoreType.DMA((9,)),
        ],
        cost_estimate=cost(COEF_US),
        compiler_params=pltpu.CompilerParams(vmem_limit_bytes=8 << 20),
    )(meta, *(pltpu.with_memory_space_constraint(array, pltpu.HBM) for array in arrays))


def stack_kernel(*refs):
    out = refs[-1]
    for k, part in enumerate(refs[:-1]):
        out[ROWS * k : ROWS * (k + 1), :] = part[...]


def stacked(*parts):
    vmem = pl.BlockSpec(memory_space=pltpu.VMEM)
    return pl.pallas_call(
        stack_kernel,
        out_shape=pltpu.VMEM((ROWS * len(parts), 128), BF16),
        in_specs=[vmem] * len(parts),
        out_specs=vmem,
        cost_estimate=cost(STACK_US),
        compiler_params=pltpu.CompilerParams(vmem_limit_bytes=4 << 20),
    )(*(pltpu.with_memory_space_constraint(part, pltpu.VMEM) for part in parts))


def near_kernel(meta, near_codes, own, sibling, far_mine, far_other, near_block, *rest):
    keep, pass_on, give, result = rest
    z, core = meta[0], meta[1] & 1
    half = z & 1
    mine = pl.ds(pl.multiple_of(half * 64, 64), 64)
    other = pl.ds(pl.multiple_of(64 - half * 64, 64), 64)
    outside = lax.select(core == 0, 0, 2)

    def body(t, carry):
        parts = []
        for i in range(2):
            code = near_codes[i, t]
            index = jnp.maximum(code, 0)
            part = index >> 5
            columns = pl.ds(pl.multiple_of((index & 31) * 128, 128), 128)
            rows = []
            for here, far in ((mine, far_mine), (other, far_other)):
                near = lax.select(part == 1, own[here, columns], sibling[here, columns])
                rows.append(lax.select(part == outside, far[:, columns], near))
            block = jnp.concatenate(rows, axis=0)
            parts.append(lax.select(code >= 0, block, jnp.zeros_like(block)))
        weights = side_by_side(near_block[t, 0], near_block[t, 1])
        here = pl.ds(pl.multiple_of(t * 128, 128), 128)
        result[:, here] = dot_nt(side_by_side(*parts), weights).astype(BF16)
        return carry

    lax.fori_loop(0, LEAVES, body, 0, unroll=8)

    def of(owner):
        start = (((owner >> 1) ^ half) & 1) * 64 + (owner & 1) * 32
        return result[pl.ds(pl.multiple_of(start, 32), 32), :]

    keep[...] = of(z)
    pass_on[...] = of(z ^ lax.select(core == 0, 3, 1))
    give[:32, :] = of(z ^ lax.select(core == 0, 1, 3))
    give[32:, :] = of(z ^ 2)


def near_partials(meta, near_codes, own, sibling, far_mine, far_other, near_block):
    smem = pl.BlockSpec(memory_space=pltpu.SMEM)
    vmem = pl.BlockSpec(memory_space=pltpu.VMEM)
    return pl.pallas_call(
        near_kernel,
        out_shape=[jax.ShapeDtypeStruct((n, 4096), BF16) for n in (32, 32, 64)],
        in_specs=[smem] * 2 + [vmem] * 5,
        out_specs=[vmem] * 3,
        scratch_shapes=[pltpu.VMEM((128, 4096), BF16)],
        cost_estimate=cost(NEAR_US),
        compiler_params=pltpu.CompilerParams(vmem_limit_bytes=12 << 20),
    )(meta, near_codes, own, sibling, far_mine, far_other, near_block)


def add_kernel(mine, taken, out):
    out[...] = (mine[...].astype(F32) + taken[32:, :].astype(F32)).astype(BF16)


def added(mine, taken):
    vmem = pl.BlockSpec(memory_space=pltpu.VMEM)
    return pl.pallas_call(
        add_kernel,
        out_shape=jax.ShapeDtypeStruct((32, 4096), BF16),
        in_specs=[vmem] * 2,
        out_specs=vmem,
        cost_estimate=cost(ADD_US),
        compiler_params=pltpu.CompilerParams(vmem_limit_bytes=4 << 20),
    )(mine, taken)


def far_kernel(leaf_codes, par_codes, held, coupling, par_coupling, transfer, out):
    lane = lax.broadcasted_iota(jnp.int32, (1, 128), 1)
    low = (lane < 64).astype(F32).astype(BF16)
    high = (lane >= 64).astype(F32).astype(BF16)

    def turned(code, wanted):
        pair = held[pl.ds(pl.multiple_of(code & ~31, 32), 32), :]
        swapped = side_by_side(pair[:, 64:], pair[:, :64])
        return lax.select((code & 1) == wanted, pair, swapped)

    def couple(codes, blocks):
        terms, weights = [], []
        for i in range(0, 8, 2):
            terms.append(turned(codes[i], 0) * low + turned(codes[i + 1], 1) * high)
            weights.append(side_by_side(blocks(i), blocks(i + 1)))
        return dot_nt(jnp.concatenate(terms, axis=1), jnp.concatenate(weights, axis=1))

    def body(q, carry):
        field = couple([par_codes[q, i] for i in range(8)], lambda i: par_coupling[q, i])
        spread = dot_nt(field.astype(BF16), transfer[pl.ds(4 * q, 4)].reshape(256, 64))
        for m in range(2):
            downs = []
            for c in (2 * m, 2 * m + 1):
                leaf = 4 * q + c
                codes = [leaf_codes[i, leaf] for i in range(8)]
                local = couple(codes, lambda i: coupling[leaf, i])
                downs.append(local + spread[:, 64 * c : 64 * (c + 1)])
            here = pl.ds(pl.multiple_of((2 * q + m) * 128, 128), 128)
            out[:, here] = side_by_side(*downs).astype(BF16)
        return carry

    lax.fori_loop(0, PARENTS, body, 0, unroll=True)


def far_down(leaf_codes, par_codes, held, coupling, par_coupling, transfer):
    smem = pl.BlockSpec(memory_space=pltpu.SMEM)
    vmem = pl.BlockSpec(memory_space=pltpu.VMEM)
    return pl.pallas_call(
        far_kernel,
        out_shape=jax.ShapeDtypeStruct((32, 2048), BF16),
        in_specs=[smem] * 2 + [vmem] * 4,
        out_specs=vmem,
        cost_estimate=cost(FAR_US),
        compiler_params=pltpu.CompilerParams(vmem_limit_bytes=18 << 20),
    )(leaf_codes, par_codes, held, coupling, par_coupling, transfer)


def sum_kernel(down, basis, keep, taken, passed, out):
    for m in range(LEAVES // 2):
        weights = diagonal(basis[2 * m], basis[2 * m + 1])
        pair = down[:, 128 * m : 128 * (m + 1)]
        result = jnp.dot(pair, weights, preferred_element_type=F32)
        here = slice(256 * m, 256 * (m + 1))
        near = keep[:, here].astype(F32) + taken[:32, here].astype(F32)
        out[:, here] = (result + (near + passed[:, here].astype(F32))).astype(BF16)


def far_and_sum(down, basis, *nears):
    vmem = pl.BlockSpec(memory_space=pltpu.VMEM)
    return pl.pallas_call(
        sum_kernel,
        out_shape=jax.ShapeDtypeStruct((32, 4096), BF16),
        in_specs=[vmem] * 5,
        out_specs=vmem,
        compiler_params=pltpu.CompilerParams(vmem_limit_bytes=8 << 20),
    )(down, basis, *nears)


def place(y, x, core):
    return (y % SIDE) * 8 + (x % SIDE) * 2 + core


def around(distance, first):
    pairs = []
    for y in range(SIDE):
        for x in range(SIDE):
            for core in range(2):
                alongx = (core == 0) == first
                to = place(y, x + distance, core) if alongx else place(y + distance, x, core)
                pairs.append((place(y, x, core), to))
    return pairs


def partners(first):
    return [
        (c * 4 + z, c * 4 + (z ^ (1 if (c % 2 == 0) == first else 3)))
        for c in range(32)
        for z in range(4)
    ]


OUTWARD = [(i, (i + (1 if i % 2 else -1)) % 32) for i in range(32)]
SWAP = [(i, i ^ 1) for i in range(32)]


def send(value, pairs, name):
    with jax.named_scope(name):
        return lax.ppermute(value, "clus", pairs)


def trade(value, first, name):
    with jax.named_scope(name):
        return lax.ppermute(value, ("clus", "rhs"), partners(first))


def joined(*parts):
    return jnp.concatenate(parts, axis=0)


def per_device(
    sources,
    leaf_basis,
    transfer,
    far_leaf,
    leaf_coupling,
    far_par,
    par_coupling,
    near_list,
    near_count,
    near_block,
):
    clus, rhs = lax.axis_index("clus"), lax.axis_index("rhs")
    meta = jnp.stack([rhs, clus]).astype(jnp.int32)
    basis = jnp.swapaxes(leaf_basis, 1, 2)
    half = lax.dynamic_slice_in_dim(sources, (rhs & 1) * 64, 64, 0)
    far_mine = send(half, OUTWARD, "halo")
    sibling = send(sources, SWAP, "sibling")
    chunk, leaf_codes, par_codes, near_codes, sources_here, near_here = coefficients(
        meta,
        sources,
        basis,
        transfer,
        far_leaf.T,
        far_par,
        near_list.T,
        near_count.reshape(1, -1),
        near_block,
    )

    across = send(chunk, around(2, True), "across")
    before = send(chunk, around(1, True), "before")
    after = send(chunk, around(-1, True), "after")
    far_other = trade(far_mine, True, "halo_half")
    own = stacked(chunk, before, after, across)
    side_b = send(own, around(1, False), "side_b")
    side_a = send(own, around(-1, False), "side_a")
    keep, pass_on, give = near_partials(
        meta, near_codes, sources_here, sibling, far_mine, far_other, near_here
    )
    taken = trade(give, True, "near_pairs")
    side_b, side_a, pass_on = lax.optimization_barrier((side_b, side_a, pass_on))
    half = own.shape[0] // 2
    far_b = send(side_b[:half], around(1, False), "far_b")
    far_a = send(side_a[half:], around(-1, False), "far_a")
    pass_on = added(pass_on, taken)
    far_b, far_a, pass_on = lax.optimization_barrier((far_b, far_a, pass_on))
    passed = trade(pass_on, False, "near_last")
    inner, far = joined(own, side_b, side_a), joined(far_b, far_a)
    held = joined(inner, far, send(inner, SWAP, "swap_inner"), send(far, SWAP, "swap_far"))
    down = far_down(leaf_codes, par_codes, held, leaf_coupling, par_coupling, transfer)
    return far_and_sum(down, basis, keep, taken, passed)


def solution(mesh):
    in_specs = (
        P(None, "clus"),
        P("clus", None, None),
        P("clus", None, None),
        P("clus", None),
        P("clus", None, None, None),
        P("clus", None),
        P("clus", None, None, None),
        P("clus", "rhs"),
        P("clus"),
        P("clus", "rhs", None, None),
    )
    return jax.shard_map(
        per_device, mesh=mesh, in_specs=in_specs, out_specs=P("rhs", "clus"), check_vma=False
    )
```

```python
import jax
import jax.numpy as jnp
from jax import lax
from jax.experimental import pallas as pl
from jax.experimental.pallas import tpu as pltpu
from jax.sharding import PartitionSpec as P

BF16 = jnp.bfloat16
F32 = jnp.float32
LEAVES = 32
PARENTS = 8
ROWS = 640
SIDE = 4
COEF_US, STACK_US, NEAR_US, FAR_US, ADD_US = 3, 4, 3, 0, 3
SIDE_STEP, FAR_STEP = 4 * ROWS, ROWS
NT = (((1,), (1,)), ((), ()))


def cost(us):
    work = int(us * 10**6)
    return pl.CostEstimate(flops=1000 * work, bytes_accessed=3 * work, transcendentals=0)


def dot_nt(a, b):
    return lax.dot_general(a, b, NT, preferred_element_type=F32)


def side_by_side(a, b):
    return jnp.concatenate([a, b], axis=1)


def diagonal(a, b):
    zeros = jnp.zeros_like(a)
    return jnp.concatenate([side_by_side(a, zeros), side_by_side(zeros, b)], axis=0)


def codes_of(index, shift, first_row, y, x, core):
    source = index >> shift
    dy, dx = ((source >> 3) - y) & 3, ((source >> 1) - x) & 3
    along_x = (source & 1) == 0
    inner, outer = jnp.where(along_x, dx, dy), jnp.where(along_x, dy, dx)

    def rank(distance):
        return jnp.where(distance == 0, 0, jnp.where(distance == 3, 1, distance + 1))

    chunk = ((source ^ core) & 1) * 16 + 4 * rank(outer) + rank(inner)
    pair = (index & ((1 << shift) - 1)) >> 1
    return (chunk * ROWS + first_row + pair * 32) | (index & 1)


def coef_kernel(meta, *refs):
    sources, basis, transfer, far_leaf, far_par, near_list, near_count, near_block = refs[:8]
    out, leaf_codes, par_codes, near_codes, own, near_here = refs[8:14]
    rows, basis_here, transfer_here, leaf_here, par_here, list_here, count_here, sems = refs[14:]
    z, clus = meta[0], meta[1]
    mine = sources.at[pl.ds(pl.multiple_of(z * 32, 32), 32), :]
    moves = (
        (mine, rows),
        (basis, basis_here),
        (transfer, transfer_here),
        (far_leaf, leaf_here),
        (far_par, par_here),
        (near_list, list_here),
        (near_count, count_here),
        (sources, own),
        (near_block, near_here),
    )
    copies = [pltpu.make_async_copy(a, b, sems.at[n]) for n, (a, b) in enumerate(moves)]
    for copy in copies:
        copy.start()
    for copy in copies[:7]:
        copy.wait()
    y, x, core = clus >> 3, (clus >> 1) & 3, clus & 1
    leaf_codes[...] = codes_of(leaf_here[...], 5, 0, y, x, core)
    par_codes[...] = codes_of(par_here[...], 3, 512, y, x, core)
    slot = z * 2 + lax.broadcasted_iota(jnp.int32, (2, LEAVES), 0)
    place = jnp.clip(list_here[...] - (clus - 1) * LEAVES, 0, 3 * LEAVES - 1)
    near_codes[...] = jnp.where(slot < count_here[...], place, -1)
    pairs = []
    for m in range(LEAVES // 2):
        weights = diagonal(basis_here[2 * m], basis_here[2 * m + 1])
        pair = dot_nt(rows[:, 256 * m : 256 * (m + 1)], weights).astype(BF16)
        out[32 * m : 32 * (m + 1), :] = pair
        pairs.append(pair)
    for n in range(PARENTS // 2):
        halves = []
        for q in (2 * n, 2 * n + 1):
            children = side_by_side(pairs[2 * q], pairs[2 * q + 1])
            weights = transfer_here[4 * q : 4 * q + 4].reshape(256, 64)
            halves.append(jnp.dot(children, weights, preferred_element_type=F32))
        out[512 + 32 * n : 512 + 32 * (n + 1), :] = side_by_side(*halves).astype(BF16)
    for copy in copies[7:]:
        copy.wait()


def coefficients(meta, *arrays):
    hbm = pl.BlockSpec(memory_space=pltpu.HBM)
    vmem = pl.BlockSpec(memory_space=pltpu.VMEM)
    tables = [(8, LEAVES), (PARENTS, 8), (2, LEAVES)]
    return pl.pallas_call(
        coef_kernel,
        out_shape=[pltpu.VMEM((ROWS, 128), BF16)]
        + [jax.ShapeDtypeStruct(table, jnp.int32) for table in tables]
        + [pltpu.VMEM((128, 4096), BF16), pltpu.VMEM((LEAVES, 2, 128, 128), BF16)],
        in_specs=[pl.BlockSpec(memory_space=pltpu.SMEM)] + [hbm] * 8,
        out_specs=[vmem] * 6,
        scratch_shapes=[
            pltpu.VMEM((32, 4096), BF16),
            pltpu.VMEM((LEAVES, 64, 128), BF16),
            pltpu.VMEM((LEAVES, 64, 64), BF16),
            pltpu.VMEM(tables[0], jnp.int32),
            pltpu.VMEM(tables[1], jnp.int32),
            pltpu.VMEM(tables[2], jnp.int32),
            pltpu.VMEM((1, LEAVES), jnp.int32),
            pltpu.SemaphoreType.DMA((9,)),
        ],
        cost_estimate=cost(COEF_US),
        compiler_params=pltpu.CompilerParams(vmem_limit_bytes=8 << 20),
    )(meta, *(pltpu.with_memory_space_constraint(array, pltpu.HBM) for array in arrays))


def fill(out, parts):
    start = 0
    for part in parts:
        out[start : start + part.shape[0], :] = part[...]
        start += part.shape[0]


def stack_kernel(*refs):
    fill(refs[-1], refs[:-1])


def stacked(*parts, us=0):
    vmem = pl.BlockSpec(memory_space=pltpu.VMEM)
    return pl.pallas_call(
        stack_kernel,
        out_shape=pltpu.VMEM((sum(part.shape[0] for part in parts), 128), BF16),
        in_specs=[vmem] * len(parts),
        out_specs=vmem,
        cost_estimate=cost(us),
        compiler_params=pltpu.CompilerParams(vmem_limit_bytes=6 << 20),
    )(*(pltpu.with_memory_space_constraint(part, pltpu.VMEM) for part in parts))


def near_kernel(meta, near_codes, own, sibling, far_mine, far_other, near_block, *rest):
    keep, pass_on, give, result = rest
    z, core = meta[0], meta[1] & 1
    half = z & 1
    mine = pl.ds(pl.multiple_of(half * 64, 64), 64)
    other = pl.ds(pl.multiple_of(64 - half * 64, 64), 64)
    outside = lax.select(core == 0, 0, 2)

    def body(t, carry):
        parts = []
        for i in range(2):
            code = near_codes[i, t]
            index = jnp.maximum(code, 0)
            part = index >> 5
            columns = pl.ds(pl.multiple_of((index & 31) * 128, 128), 128)
            rows = []
            for here, far in ((mine, far_mine), (other, far_other)):
                near = lax.select(part == 1, own[here, columns], sibling[here, columns])
                rows.append(lax.select(part == outside, far[:, columns], near))
            block = jnp.concatenate(rows, axis=0)
            parts.append(lax.select(code >= 0, block, jnp.zeros_like(block)))
        weights = side_by_side(near_block[t, 0], near_block[t, 1])
        here = pl.ds(pl.multiple_of(t * 128, 128), 128)
        result[:, here] = dot_nt(side_by_side(*parts), weights).astype(BF16)
        return carry

    lax.fori_loop(0, LEAVES, body, 0, unroll=8)

    def of(owner):
        start = (((owner >> 1) ^ half) & 1) * 64 + (owner & 1) * 32
        return result[pl.ds(pl.multiple_of(start, 32), 32), :]

    keep[...] = of(z)
    pass_on[...] = of(z ^ lax.select(core == 0, 3, 1))
    give[:32, :] = of(z ^ lax.select(core == 0, 1, 3))
    give[32:, :] = of(z ^ 2)


def near_partials(meta, near_codes, own, sibling, far_mine, far_other, near_block):
    smem = pl.BlockSpec(memory_space=pltpu.SMEM)
    vmem = pl.BlockSpec(memory_space=pltpu.VMEM)
    return pl.pallas_call(
        near_kernel,
        out_shape=[jax.ShapeDtypeStruct((n, 4096), BF16) for n in (32, 32, 64)],
        in_specs=[smem] * 2 + [vmem] * 5,
        out_specs=[vmem] * 3,
        scratch_shapes=[pltpu.VMEM((128, 4096), BF16)],
        cost_estimate=cost(NEAR_US),
        compiler_params=pltpu.CompilerParams(vmem_limit_bytes=12 << 20),
    )(meta, near_codes, own, sibling, far_mine, far_other, near_block)


def add_kernel(mine, taken, out):
    out[...] = (mine[...].astype(F32) + taken[32:, :].astype(F32)).astype(BF16)


def added(mine, taken):
    vmem = pl.BlockSpec(memory_space=pltpu.VMEM)
    return pl.pallas_call(
        add_kernel,
        out_shape=jax.ShapeDtypeStruct((32, 4096), BF16),
        in_specs=[vmem] * 2,
        out_specs=vmem,
        cost_estimate=cost(ADD_US),
        compiler_params=pltpu.CompilerParams(vmem_limit_bytes=4 << 20),
    )(mine, taken)


def far_kernel(leaf_codes, par_codes, *refs):
    coupling, par_coupling, transfer, out, held = refs[-5:]
    fill(held, refs[:-5])
    lane = lax.broadcasted_iota(jnp.int32, (1, 128), 1)
    low = (lane < 64).astype(F32).astype(BF16)
    high = (lane >= 64).astype(F32).astype(BF16)

    def turned(code, wanted):
        pair = held[pl.ds(pl.multiple_of(code & ~31, 32), 32), :]
        swapped = side_by_side(pair[:, 64:], pair[:, :64])
        return lax.select((code & 1) == wanted, pair, swapped)

    def couple(codes, blocks):
        terms, weights = [], []
        for i in range(0, 8, 2):
            terms.append(turned(codes[i], 0) * low + turned(codes[i + 1], 1) * high)
            weights.append(side_by_side(blocks(i), blocks(i + 1)))
        return dot_nt(jnp.concatenate(terms, axis=1), jnp.concatenate(weights, axis=1))

    def body(q, carry):
        field = couple([par_codes[q, i] for i in range(8)], lambda i: par_coupling[q, i])
        spread = dot_nt(field.astype(BF16), transfer[pl.ds(4 * q, 4)].reshape(256, 64))
        for m in range(2):
            downs = []
            for c in (2 * m, 2 * m + 1):
                leaf = 4 * q + c
                codes = [leaf_codes[i, leaf] for i in range(8)]
                local = couple(codes, lambda i: coupling[leaf, i])
                downs.append(local + spread[:, 64 * c : 64 * (c + 1)])
            here = pl.ds(pl.multiple_of((2 * q + m) * 128, 128), 128)
            out[:, here] = side_by_side(*downs).astype(BF16)
        return carry

    lax.fori_loop(0, PARENTS, body, 0, unroll=True)


def far_down(leaf_codes, par_codes, gathered, coupling, par_coupling, transfer):
    smem = pl.BlockSpec(memory_space=pltpu.SMEM)
    vmem = pl.BlockSpec(memory_space=pltpu.VMEM)
    gathered = [pltpu.with_memory_space_constraint(part, pltpu.VMEM) for part in gathered]
    return pl.pallas_call(
        far_kernel,
        out_shape=jax.ShapeDtypeStruct((32, 2048), BF16),
        in_specs=[smem] * 2 + [vmem] * (len(gathered) + 3),
        out_specs=vmem,
        scratch_shapes=[pltpu.VMEM((32 * ROWS, 128), BF16)],
        cost_estimate=cost(FAR_US),
        compiler_params=pltpu.CompilerParams(vmem_limit_bytes=22 << 20),
    )(leaf_codes, par_codes, *gathered, coupling, par_coupling, transfer)


def sum_kernel(down, basis, keep, taken, passed, out):
    for m in range(LEAVES // 2):
        weights = diagonal(basis[2 * m], basis[2 * m + 1])
        pair = down[:, 128 * m : 128 * (m + 1)]
        result = jnp.dot(pair, weights, preferred_element_type=F32)
        here = slice(256 * m, 256 * (m + 1))
        near = keep[:, here].astype(F32) + taken[:32, here].astype(F32)
        out[:, here] = (result + (near + passed[:, here].astype(F32))).astype(BF16)


def far_and_sum(down, basis, *nears):
    vmem = pl.BlockSpec(memory_space=pltpu.VMEM)
    return pl.pallas_call(
        sum_kernel,
        out_shape=jax.ShapeDtypeStruct((32, 4096), BF16),
        in_specs=[vmem] * 5,
        out_specs=vmem,
        compiler_params=pltpu.CompilerParams(vmem_limit_bytes=8 << 20),
    )(down, basis, *nears)


def place(y, x, core):
    return (y % SIDE) * 8 + (x % SIDE) * 2 + core


def around(distance, first):
    pairs = []
    for y in range(SIDE):
        for x in range(SIDE):
            for core in range(2):
                alongx = (core == 0) == first
                to = place(y, x + distance, core) if alongx else place(y + distance, x, core)
                pairs.append((place(y, x, core), to))
    return pairs


def partners(first):
    return [
        (c * 4 + z, c * 4 + (z ^ (1 if (c % 2 == 0) == first else 3)))
        for c in range(32)
        for z in range(4)
    ]


OUTWARD = [(i, (i + (1 if i % 2 else -1)) % 32) for i in range(32)]
SWAP = [(i, i ^ 1) for i in range(32)]


def send(value, pairs, name):
    with jax.named_scope(name):
        return lax.ppermute(value, "clus", pairs)


def trade(value, first, name):
    with jax.named_scope(name):
        return lax.ppermute(value, ("clus", "rhs"), partners(first))


def per_device(
    sources,
    leaf_basis,
    transfer,
    far_leaf,
    leaf_coupling,
    far_par,
    par_coupling,
    near_list,
    near_count,
    near_block,
):
    clus, rhs = lax.axis_index("clus"), lax.axis_index("rhs")
    meta = jnp.stack([rhs, clus]).astype(jnp.int32)
    basis = jnp.swapaxes(leaf_basis, 1, 2)
    half = lax.dynamic_slice_in_dim(sources, (rhs & 1) * 64, 64, 0)
    far_mine = send(half, OUTWARD, "halo")
    sibling = send(sources, SWAP, "sibling")
    chunk, leaf_codes, par_codes, near_codes, sources_here, near_here = coefficients(
        meta,
        sources,
        basis,
        transfer,
        far_leaf.T,
        far_par,
        near_list.T,
        near_count.reshape(1, -1),
        near_block,
    )

    across = send(chunk, around(2, True), "across")
    before = send(chunk, around(1, True), "before")
    after = send(chunk, around(-1, True), "after")
    far_other = trade(far_mine, True, "halo_half")
    own = stacked(chunk, before, after, across, us=STACK_US)
    side_b = send(own, around(1, False), "side_b")
    side_a = send(own, around(-1, False), "side_a")
    keep, pass_on, give = near_partials(
        meta, near_codes, sources_here, sibling, far_mine, far_other, near_here
    )
    taken = trade(give, True, "near_pairs")
    own_other = send(own, SWAP, "swap_own")
    side_b, side_a, pass_on, own_other = lax.optimization_barrier(
        (side_b, side_a, pass_on, own_other)
    )
    half = own.shape[0] // 2
    far_b = send(side_b[:half], around(1, False), "far_b")
    far_a = send(side_a[half:], around(-1, False), "far_a")
    pass_on = added(pass_on, taken)
    passed = trade(pass_on, False, "near_last")
    far_b, far_a, pass_on = lax.optimization_barrier((far_b, far_a, pass_on))
    def swapped(name, *parts, step):
        pieces = [part[k : k + step] for part in parts for k in range(0, part.shape[0], step)]
        return tuple(send(piece, SWAP, name) for piece in pieces)

    mine = (own, side_b, side_a, far_b, far_a)
    inner = (own_other,) + swapped("swap_side", side_b, side_a, step=SIDE_STEP)
    outer = swapped("swap_far", far_b, far_a, step=FAR_STEP)
    gathered = mine + inner + outer
    down = far_down(leaf_codes, par_codes, gathered, leaf_coupling, par_coupling, transfer)
    return far_and_sum(down, basis, keep, taken, passed)


def solution(mesh):
    in_specs = (
        P(None, "clus"),
        P("clus", None, None),
        P("clus", None, None),
        P("clus", None),
        P("clus", None, None, None),
        P("clus", None),
        P("clus", None, None, None),
        P("clus", "rhs"),
        P("clus"),
        P("clus", "rhs", None, None),
    )
    return jax.shard_map(
        per_device, mesh=mesh, in_specs=in_specs, out_specs=P("rhs", "clus"), check_vma=False
    )
```

```python
import jax
import jax.numpy as jnp
from jax import lax
from jax.experimental import pallas as pl
from jax.experimental.pallas import tpu as pltpu
from jax.sharding import PartitionSpec as P

BF16 = jnp.bfloat16
F32 = jnp.float32
LEAVES = 32
PARENTS = 8
ROWS = 640
SIDE = 4
COEF_US, STACK_US, NEAR_US, FAR_US, ADD_US = 3, 4, 3, 0, 3
SIDE_STEP, FAR_STEP = 4 * ROWS, ROWS
NT = (((1,), (1,)), ((), ()))


def cost(us):
    work = int(us * 10**6)
    return pl.CostEstimate(flops=1000 * work, bytes_accessed=3 * work, transcendentals=0)


def dot_nt(a, b):
    return lax.dot_general(a, b, NT, preferred_element_type=F32)


def side_by_side(a, b):
    return jnp.concatenate([a, b], axis=1)


def diagonal(a, b):
    zeros = jnp.zeros_like(a)
    return jnp.concatenate([side_by_side(a, zeros), side_by_side(zeros, b)], axis=0)


def codes_of(index, shift, first_row, y, x, core):
    source = index >> shift
    dy, dx = ((source >> 3) - y) & 3, ((source >> 1) - x) & 3
    along_x = (source & 1) == 0
    inner, outer = jnp.where(along_x, dx, dy), jnp.where(along_x, dy, dx)

    def rank(distance):
        return jnp.where(distance == 0, 0, jnp.where(distance == 3, 1, distance + 1))

    chunk = ((source ^ core) & 1) * 16 + 4 * rank(outer) + rank(inner)
    pair = (index & ((1 << shift) - 1)) >> 1
    return (chunk * ROWS + first_row + pair * 32) | (index & 1)


def coef_kernel(meta, *refs):
    sources, basis, transfer, far_leaf, far_par, near_list, near_count, near_block = refs[:8]
    out, leaf_codes, par_codes, near_codes, own, near_here = refs[8:14]
    rows, basis_here, transfer_here, leaf_here, par_here, list_here, count_here, sems = refs[14:]
    z, clus = meta[0], meta[1]
    mine = sources.at[pl.ds(pl.multiple_of(z * 32, 32), 32), :]
    moves = (
        (mine, rows),
        (basis, basis_here),
        (transfer, transfer_here),
        (far_leaf, leaf_here),
        (far_par, par_here),
        (near_list, list_here),
        (near_count, count_here),
        (sources, own),
        (near_block, near_here),
    )
    copies = [pltpu.make_async_copy(a, b, sems.at[n]) for n, (a, b) in enumerate(moves)]
    for copy in copies[:7]:
        copy.start()
    for copy in copies[:2]:
        copy.wait()
    for copy in copies[7:]:
        copy.start()
    for copy in copies[3:7]:
        copy.wait()
    y, x, core = clus >> 3, (clus >> 1) & 3, clus & 1
    leaf_codes[...] = codes_of(leaf_here[...], 5, 0, y, x, core)
    par_codes[...] = codes_of(par_here[...], 3, 512, y, x, core)
    slot = z * 2 + lax.broadcasted_iota(jnp.int32, (2, LEAVES), 0)
    place = jnp.clip(list_here[...] - (clus - 1) * LEAVES, 0, 3 * LEAVES - 1)
    near_codes[...] = jnp.where(slot < count_here[...], place, -1)
    pairs = []
    for m in range(LEAVES // 2):
        weights = diagonal(basis_here[2 * m], basis_here[2 * m + 1])
        pair = dot_nt(rows[:, 256 * m : 256 * (m + 1)], weights).astype(BF16)
        out[32 * m : 32 * (m + 1), :] = pair
        pairs.append(pair)
    copies[2].wait()
    for n in range(PARENTS // 2):
        halves = []
        for q in (2 * n, 2 * n + 1):
            children = side_by_side(pairs[2 * q], pairs[2 * q + 1])
            weights = transfer_here[4 * q : 4 * q + 4].reshape(256, 64)
            halves.append(jnp.dot(children, weights, preferred_element_type=F32))
        out[512 + 32 * n : 512 + 32 * (n + 1), :] = side_by_side(*halves).astype(BF16)
    for copy in copies[7:]:
        copy.wait()


def coefficients(meta, *arrays):
    hbm = pl.BlockSpec(memory_space=pltpu.HBM)
    vmem = pl.BlockSpec(memory_space=pltpu.VMEM)
    tables = [(8, LEAVES), (PARENTS, 8), (2, LEAVES)]
    return pl.pallas_call(
        coef_kernel,
        out_shape=[pltpu.VMEM((ROWS, 128), BF16)]
        + [jax.ShapeDtypeStruct(table, jnp.int32) for table in tables]
        + [pltpu.VMEM((128, 4096), BF16), pltpu.VMEM((LEAVES, 2, 128, 128), BF16)],
        in_specs=[pl.BlockSpec(memory_space=pltpu.SMEM)] + [hbm] * 8,
        out_specs=[vmem] * 6,
        scratch_shapes=[
            pltpu.VMEM((32, 4096), BF16),
            pltpu.VMEM((LEAVES, 64, 128), BF16),
            pltpu.VMEM((LEAVES, 64, 64), BF16),
            pltpu.VMEM(tables[0], jnp.int32),
            pltpu.VMEM(tables[1], jnp.int32),
            pltpu.VMEM(tables[2], jnp.int32),
            pltpu.VMEM((1, LEAVES), jnp.int32),
            pltpu.SemaphoreType.DMA((9,)),
        ],
        cost_estimate=cost(COEF_US),
        compiler_params=pltpu.CompilerParams(vmem_limit_bytes=8 << 20),
    )(meta, *(pltpu.with_memory_space_constraint(array, pltpu.HBM) for array in arrays))


def fill(out, parts):
    start = 0
    for part in parts:
        out[start : start + part.shape[0], :] = part[...]
        start += part.shape[0]


def stack_kernel(*refs):
    fill(refs[-1], refs[:-1])


def stacked(*parts, us=0):
    vmem = pl.BlockSpec(memory_space=pltpu.VMEM)
    return pl.pallas_call(
        stack_kernel,
        out_shape=pltpu.VMEM((sum(part.shape[0] for part in parts), 128), BF16),
        in_specs=[vmem] * len(parts),
        out_specs=vmem,
        cost_estimate=cost(us),
        compiler_params=pltpu.CompilerParams(vmem_limit_bytes=6 << 20),
    )(*(pltpu.with_memory_space_constraint(part, pltpu.VMEM) for part in parts))


def near_kernel(meta, near_codes, own, sibling, far_mine, far_other, near_block, *rest):
    keep, pass_on, give, result = rest
    z, core = meta[0], meta[1] & 1
    half = z & 1
    mine = pl.ds(pl.multiple_of(half * 64, 64), 64)
    other = pl.ds(pl.multiple_of(64 - half * 64, 64), 64)
    outside = lax.select(core == 0, 0, 2)

    def body(t, carry):
        parts = []
        for i in range(2):
            code = near_codes[i, t]
            index = jnp.maximum(code, 0)
            part = index >> 5
            columns = pl.ds(pl.multiple_of((index & 31) * 128, 128), 128)
            rows = []
            for here, far in ((mine, far_mine), (other, far_other)):
                near = lax.select(part == 1, own[here, columns], sibling[here, columns])
                rows.append(lax.select(part == outside, far[:, columns], near))
            block = jnp.concatenate(rows, axis=0)
            parts.append(lax.select(code >= 0, block, jnp.zeros_like(block)))
        weights = side_by_side(near_block[t, 0], near_block[t, 1])
        here = pl.ds(pl.multiple_of(t * 128, 128), 128)
        result[:, here] = dot_nt(side_by_side(*parts), weights).astype(BF16)
        return carry

    lax.fori_loop(0, LEAVES, body, 0, unroll=8)

    def of(owner):
        start = (((owner >> 1) ^ half) & 1) * 64 + (owner & 1) * 32
        return result[pl.ds(pl.multiple_of(start, 32), 32), :]

    keep[...] = of(z)
    pass_on[...] = of(z ^ lax.select(core == 0, 3, 1))
    give[:32, :] = of(z ^ lax.select(core == 0, 1, 3))
    give[32:, :] = of(z ^ 2)


def near_partials(meta, near_codes, own, sibling, far_mine, far_other, near_block):
    smem = pl.BlockSpec(memory_space=pltpu.SMEM)
    vmem = pl.BlockSpec(memory_space=pltpu.VMEM)
    return pl.pallas_call(
        near_kernel,
        out_shape=[jax.ShapeDtypeStruct((n, 4096), BF16) for n in (32, 32, 64)],
        in_specs=[smem] * 2 + [vmem] * 5,
        out_specs=[vmem] * 3,
        scratch_shapes=[pltpu.VMEM((128, 4096), BF16)],
        cost_estimate=cost(NEAR_US),
        compiler_params=pltpu.CompilerParams(vmem_limit_bytes=12 << 20),
    )(meta, near_codes, own, sibling, far_mine, far_other, near_block)


def add_kernel(mine, taken, out):
    out[...] = (mine[...].astype(F32) + taken[32:, :].astype(F32)).astype(BF16)


def added(mine, taken):
    vmem = pl.BlockSpec(memory_space=pltpu.VMEM)
    return pl.pallas_call(
        add_kernel,
        out_shape=jax.ShapeDtypeStruct((32, 4096), BF16),
        in_specs=[vmem] * 2,
        out_specs=vmem,
        cost_estimate=cost(ADD_US),
        compiler_params=pltpu.CompilerParams(vmem_limit_bytes=4 << 20),
    )(mine, taken)


def far_kernel(leaf_codes, par_codes, *refs):
    coupling, par_coupling, transfer, out, held = refs[-5:]
    fill(held, refs[:-5])
    lane = lax.broadcasted_iota(jnp.int32, (1, 128), 1)
    low = (lane < 64).astype(F32).astype(BF16)
    high = (lane >= 64).astype(F32).astype(BF16)

    def turned(code, wanted):
        pair = held[pl.ds(pl.multiple_of(code & ~31, 32), 32), :]
        swapped = side_by_side(pair[:, 64:], pair[:, :64])
        return lax.select((code & 1) == wanted, pair, swapped)

    def couple(codes, blocks):
        terms, weights = [], []
        for i in range(0, 8, 2):
            terms.append(turned(codes[i], 0) * low + turned(codes[i + 1], 1) * high)
            weights.append(side_by_side(blocks(i), blocks(i + 1)))
        return dot_nt(jnp.concatenate(terms, axis=1), jnp.concatenate(weights, axis=1))

    def body(q, carry):
        field = couple([par_codes[q, i] for i in range(8)], lambda i: par_coupling[q, i])
        spread = dot_nt(field.astype(BF16), transfer[pl.ds(4 * q, 4)].reshape(256, 64))
        for m in range(2):
            downs = []
            for c in (2 * m, 2 * m + 1):
                leaf = 4 * q + c
                codes = [leaf_codes[i, leaf] for i in range(8)]
                local = couple(codes, lambda i: coupling[leaf, i])
                downs.append(local + spread[:, 64 * c : 64 * (c + 1)])
            here = pl.ds(pl.multiple_of((2 * q + m) * 128, 128), 128)
            out[:, here] = side_by_side(*downs).astype(BF16)
        return carry

    lax.fori_loop(0, PARENTS, body, 0, unroll=True)


def far_down(leaf_codes, par_codes, gathered, coupling, par_coupling, transfer):
    smem = pl.BlockSpec(memory_space=pltpu.SMEM)
    vmem = pl.BlockSpec(memory_space=pltpu.VMEM)
    gathered = [pltpu.with_memory_space_constraint(part, pltpu.VMEM) for part in gathered]
    return pl.pallas_call(
        far_kernel,
        out_shape=jax.ShapeDtypeStruct((32, 2048), BF16),
        in_specs=[smem] * 2 + [vmem] * (len(gathered) + 3),
        out_specs=vmem,
        scratch_shapes=[pltpu.VMEM((32 * ROWS, 128), BF16)],
        cost_estimate=cost(FAR_US),
        compiler_params=pltpu.CompilerParams(vmem_limit_bytes=22 << 20),
    )(leaf_codes, par_codes, *gathered, coupling, par_coupling, transfer)


def sum_kernel(down, basis, keep, taken, passed, out):
    for m in range(LEAVES // 2):
        weights = diagonal(basis[2 * m], basis[2 * m + 1])
        pair = down[:, 128 * m : 128 * (m + 1)]
        result = jnp.dot(pair, weights, preferred_element_type=F32)
        here = slice(256 * m, 256 * (m + 1))
        near = keep[:, here].astype(F32) + taken[:32, here].astype(F32)
        out[:, here] = (result + (near + passed[:, here].astype(F32))).astype(BF16)


def far_and_sum(down, basis, *nears):
    vmem = pl.BlockSpec(memory_space=pltpu.VMEM)
    return pl.pallas_call(
        sum_kernel,
        out_shape=jax.ShapeDtypeStruct((32, 4096), BF16),
        in_specs=[vmem] * 5,
        out_specs=vmem,
        compiler_params=pltpu.CompilerParams(vmem_limit_bytes=8 << 20),
    )(down, basis, *nears)


def place(y, x, core):
    return (y % SIDE) * 8 + (x % SIDE) * 2 + core


def around(distance, first):
    pairs = []
    for y in range(SIDE):
        for x in range(SIDE):
            for core in range(2):
                alongx = (core == 0) == first
                to = place(y, x + distance, core) if alongx else place(y + distance, x, core)
                pairs.append((place(y, x, core), to))
    return pairs


def partners(first):
    return [
        (c * 4 + z, c * 4 + (z ^ (1 if (c % 2 == 0) == first else 3)))
        for c in range(32)
        for z in range(4)
    ]


OUTWARD = [(i, (i + (1 if i % 2 else -1)) % 32) for i in range(32)]
SWAP = [(i, i ^ 1) for i in range(32)]


def send(value, pairs, name):
    with jax.named_scope(name):
        return lax.ppermute(value, "clus", pairs)


def trade(value, first, name):
    with jax.named_scope(name):
        return lax.ppermute(value, ("clus", "rhs"), partners(first))


def per_device(
    sources,
    leaf_basis,
    transfer,
    far_leaf,
    leaf_coupling,
    far_par,
    par_coupling,
    near_list,
    near_count,
    near_block,
):
    clus, rhs = lax.axis_index("clus"), lax.axis_index("rhs")
    meta = jnp.stack([rhs, clus]).astype(jnp.int32)
    basis = jnp.swapaxes(leaf_basis, 1, 2)
    half = lax.dynamic_slice_in_dim(sources, (rhs & 1) * 64, 64, 0)
    far_mine = send(half, OUTWARD, "halo")
    sibling = send(sources, SWAP, "sibling")
    chunk, leaf_codes, par_codes, near_codes, sources_here, near_here = coefficients(
        meta,
        sources,
        basis,
        transfer,
        far_leaf.T,
        far_par,
        near_list.T,
        near_count.reshape(1, -1),
        near_block,
    )

    across = send(chunk, around(2, True), "across")
    before = send(chunk, around(1, True), "before")
    after = send(chunk, around(-1, True), "after")
    far_other = trade(far_mine, True, "halo_half")
    own = stacked(chunk, before, after, across, us=STACK_US)
    side_b = send(own, around(1, False), "side_b")
    side_a = send(own, around(-1, False), "side_a")
    keep, pass_on, give = near_partials(
        meta, near_codes, sources_here, sibling, far_mine, far_other, near_here
    )
    taken = trade(give, True, "near_pairs")
    own_other = send(own, SWAP, "swap_own")
    side_b, side_a, pass_on, own_other = lax.optimization_barrier(
        (side_b, side_a, pass_on, own_other)
    )
    half = own.shape[0] // 2
    far_b = send(side_b[:half], around(1, False), "far_b")
    far_a = send(side_a[half:], around(-1, False), "far_a")
    pass_on = added(pass_on, taken)
    passed = trade(pass_on, False, "near_last")
    far_b, far_a, pass_on = lax.optimization_barrier((far_b, far_a, pass_on))
    def swapped(name, *parts, step):
        pieces = [part[k : k + step] for part in parts for k in range(0, part.shape[0], step)]
        return tuple(send(piece, SWAP, name) for piece in pieces)

    mine = (own, side_b, side_a, far_b, far_a)
    inner = (own_other,) + swapped("swap_side", side_b, side_a, step=SIDE_STEP)
    outer = swapped("swap_far", far_b, far_a, step=FAR_STEP)
    gathered = mine + inner + outer
    down = far_down(leaf_codes, par_codes, gathered, leaf_coupling, par_coupling, transfer)
    return far_and_sum(down, basis, keep, taken, passed)


def solution(mesh):
    in_specs = (
        P(None, "clus"),
        P("clus", None, None),
        P("clus", None, None),
        P("clus", None),
        P("clus", None, None, None),
        P("clus", None),
        P("clus", None, None, None),
        P("clus", "rhs"),
        P("clus"),
        P("clus", "rhs", None, None),
    )
    return jax.shard_map(
        per_device, mesh=mesh, in_specs=in_specs, out_specs=P("rhs", "clus"), check_vma=False
    )
```

```python
import jax
import jax.numpy as jnp
from jax import lax
from jax.experimental import pallas as pl
from jax.experimental.pallas import tpu as pltpu
from jax.sharding import PartitionSpec as P

BF16 = jnp.bfloat16
F32 = jnp.float32
LEAVES = 32
PARENTS = 8
ROWS = 640
SIDE = 4
COEF_US, STACK_US, NEAR_US, FAR_US, ADD_US = 3, 4, 3, 0, 3
SIDE_STEP, FAR_STEP = 4 * ROWS, ROWS
NT = (((1,), (1,)), ((), ()))


def cost(us):
    work = int(us * 10**6)
    return pl.CostEstimate(flops=1000 * work, bytes_accessed=3 * work, transcendentals=0)


def dot_nt(a, b):
    return lax.dot_general(a, b, NT, preferred_element_type=F32)


def side_by_side(a, b):
    return jnp.concatenate([a, b], axis=1)


def diagonal(a, b):
    zeros = jnp.zeros_like(a)
    return jnp.concatenate([side_by_side(a, zeros), side_by_side(zeros, b)], axis=0)


def codes_of(index, shift, first_row, y, x, core):
    source = index >> shift
    dy, dx = ((source >> 3) - y) & 3, ((source >> 1) - x) & 3
    along_x = (source & 1) == 0
    inner, outer = jnp.where(along_x, dx, dy), jnp.where(along_x, dy, dx)

    def rank(distance):
        return jnp.where(distance == 0, 0, jnp.where(distance == 3, 1, distance + 1))

    chunk = ((source ^ core) & 1) * 16 + 4 * rank(outer) + rank(inner)
    pair = (index & ((1 << shift) - 1)) >> 1
    return (chunk * ROWS + first_row + pair * 32) | (index & 1)


def coef_kernel(meta, *refs):
    sources, basis, transfer, far_leaf, far_par, near_list, near_count, near_block = refs[:8]
    out, leaf_codes, par_codes, near_codes, own, near_here = refs[8:14]
    rows, basis_here, transfer_here, leaf_here, par_here, list_here, count_here, sems = refs[14:]
    z, clus = meta[0], meta[1]
    mine = sources.at[pl.ds(pl.multiple_of(z * 32, 32), 32), :]
    moves = (
        (mine, rows),
        (basis, basis_here),
        (transfer, transfer_here),
        (far_leaf, leaf_here),
        (far_par, par_here),
        (near_list, list_here),
        (near_count, count_here),
        (sources, own),
        (near_block, near_here),
    )
    copies = [pltpu.make_async_copy(a, b, sems.at[n]) for n, (a, b) in enumerate(moves)]
    for copy in copies[:7]:
        copy.start()
    for copy in copies[:2]:
        copy.wait()
    for copy in copies[7:]:
        copy.start()
    pairs = []
    for m in range(LEAVES // 2):
        weights = diagonal(basis_here[2 * m], basis_here[2 * m + 1])
        pair = dot_nt(rows[:, 256 * m : 256 * (m + 1)], weights).astype(BF16)
        out[32 * m : 32 * (m + 1), :] = pair
        pairs.append(pair)
    copies[2].wait()
    for n in range(PARENTS // 2):
        halves = []
        for q in (2 * n, 2 * n + 1):
            children = side_by_side(pairs[2 * q], pairs[2 * q + 1])
            weights = transfer_here[4 * q : 4 * q + 4].reshape(256, 64)
            halves.append(jnp.dot(children, weights, preferred_element_type=F32))
        out[512 + 32 * n : 512 + 32 * (n + 1), :] = side_by_side(*halves).astype(BF16)
    for copy in copies[3:7]:
        copy.wait()
    y, x, core = clus >> 3, (clus >> 1) & 3, clus & 1
    leaf_codes[...] = codes_of(leaf_here[...], 5, 0, y, x, core)
    par_codes[...] = codes_of(par_here[...], 3, 512, y, x, core)
    slot = z * 2 + lax.broadcasted_iota(jnp.int32, (2, LEAVES), 0)
    place = jnp.clip(list_here[...] - (clus - 1) * LEAVES, 0, 3 * LEAVES - 1)
    near_codes[...] = jnp.where(slot < count_here[...], place, -1)
    for copy in copies[7:]:
        copy.wait()


def coefficients(meta, *arrays):
    hbm = pl.BlockSpec(memory_space=pltpu.HBM)
    vmem = pl.BlockSpec(memory_space=pltpu.VMEM)
    tables = [(8, LEAVES), (PARENTS, 8), (2, LEAVES)]
    return pl.pallas_call(
        coef_kernel,
        out_shape=[pltpu.VMEM((ROWS, 128), BF16)]
        + [jax.ShapeDtypeStruct(table, jnp.int32) for table in tables]
        + [pltpu.VMEM((128, 4096), BF16), pltpu.VMEM((LEAVES, 2, 128, 128), BF16)],
        in_specs=[pl.BlockSpec(memory_space=pltpu.SMEM)] + [hbm] * 8,
        out_specs=[vmem] * 6,
        scratch_shapes=[
            pltpu.VMEM((32, 4096), BF16),
            pltpu.VMEM((LEAVES, 64, 128), BF16),
            pltpu.VMEM((LEAVES, 64, 64), BF16),
            pltpu.VMEM(tables[0], jnp.int32),
            pltpu.VMEM(tables[1], jnp.int32),
            pltpu.VMEM(tables[2], jnp.int32),
            pltpu.VMEM((1, LEAVES), jnp.int32),
            pltpu.SemaphoreType.DMA((9,)),
        ],
        cost_estimate=cost(COEF_US),
        compiler_params=pltpu.CompilerParams(vmem_limit_bytes=8 << 20),
    )(meta, *(pltpu.with_memory_space_constraint(array, pltpu.HBM) for array in arrays))


def fill(out, parts):
    start = 0
    for part in parts:
        out[start : start + part.shape[0], :] = part[...]
        start += part.shape[0]


def stack_kernel(*refs):
    fill(refs[-1], refs[:-1])


def stacked(*parts, us=0):
    vmem = pl.BlockSpec(memory_space=pltpu.VMEM)
    return pl.pallas_call(
        stack_kernel,
        out_shape=pltpu.VMEM((sum(part.shape[0] for part in parts), 128), BF16),
        in_specs=[vmem] * len(parts),
        out_specs=vmem,
        cost_estimate=cost(us),
        compiler_params=pltpu.CompilerParams(vmem_limit_bytes=6 << 20),
    )(*(pltpu.with_memory_space_constraint(part, pltpu.VMEM) for part in parts))


def near_kernel(meta, near_codes, own, sibling, far_mine, far_other, near_block, *rest):
    keep, pass_on, give, result = rest
    z, core = meta[0], meta[1] & 1
    half = z & 1
    mine = pl.ds(pl.multiple_of(half * 64, 64), 64)
    other = pl.ds(pl.multiple_of(64 - half * 64, 64), 64)
    outside = lax.select(core == 0, 0, 2)

    def body(t, carry):
        parts = []
        for i in range(2):
            code = near_codes[i, t]
            index = jnp.maximum(code, 0)
            part = index >> 5
            columns = pl.ds(pl.multiple_of((index & 31) * 128, 128), 128)
            rows = []
            for here, far in ((mine, far_mine), (other, far_other)):
                near = lax.select(part == 1, own[here, columns], sibling[here, columns])
                rows.append(lax.select(part == outside, far[:, columns], near))
            block = jnp.concatenate(rows, axis=0)
            parts.append(lax.select(code >= 0, block, jnp.zeros_like(block)))
        weights = side_by_side(near_block[t, 0], near_block[t, 1])
        here = pl.ds(pl.multiple_of(t * 128, 128), 128)
        result[:, here] = dot_nt(side_by_side(*parts), weights).astype(BF16)
        return carry

    lax.fori_loop(0, LEAVES, body, 0, unroll=8)

    def of(owner):
        start = (((owner >> 1) ^ half) & 1) * 64 + (owner & 1) * 32
        return result[pl.ds(pl.multiple_of(start, 32), 32), :]

    keep[...] = of(z)
    pass_on[...] = of(z ^ lax.select(core == 0, 3, 1))
    give[:32, :] = of(z ^ lax.select(core == 0, 1, 3))
    give[32:, :] = of(z ^ 2)


def near_partials(meta, near_codes, own, sibling, far_mine, far_other, near_block):
    smem = pl.BlockSpec(memory_space=pltpu.SMEM)
    vmem = pl.BlockSpec(memory_space=pltpu.VMEM)
    return pl.pallas_call(
        near_kernel,
        out_shape=[jax.ShapeDtypeStruct((n, 4096), BF16) for n in (32, 32, 64)],
        in_specs=[smem] * 2 + [vmem] * 5,
        out_specs=[vmem] * 3,
        scratch_shapes=[pltpu.VMEM((128, 4096), BF16)],
        cost_estimate=cost(NEAR_US),
        compiler_params=pltpu.CompilerParams(vmem_limit_bytes=12 << 20),
    )(meta, near_codes, own, sibling, far_mine, far_other, near_block)


def add_kernel(mine, taken, out):
    out[...] = (mine[...].astype(F32) + taken[32:, :].astype(F32)).astype(BF16)


def added(mine, taken):
    vmem = pl.BlockSpec(memory_space=pltpu.VMEM)
    return pl.pallas_call(
        add_kernel,
        out_shape=jax.ShapeDtypeStruct((32, 4096), BF16),
        in_specs=[vmem] * 2,
        out_specs=vmem,
        cost_estimate=cost(ADD_US),
        compiler_params=pltpu.CompilerParams(vmem_limit_bytes=4 << 20),
    )(mine, taken)


def far_kernel(leaf_codes, par_codes, *refs):
    coupling, par_coupling, transfer, out, held = refs[-5:]
    fill(held, refs[:-5])
    lane = lax.broadcasted_iota(jnp.int32, (32, 128), 1)
    first = lane < 64

    def turned(code, wanted):
        pair = held[pl.ds(pl.multiple_of(code & ~31, 32), 32), :]
        swapped = side_by_side(pair[:, 64:], pair[:, :64])
        return lax.select((code & 1) == wanted, pair, swapped)

    def couple(codes, blocks):
        terms, weights = [], []
        for i in range(0, 8, 2):
            terms.append(jnp.where(first, turned(codes[i], 0), turned(codes[i + 1], 1)))
            weights.append(side_by_side(blocks(i), blocks(i + 1)))
        return dot_nt(jnp.concatenate(terms, axis=1), jnp.concatenate(weights, axis=1))

    def body(q, carry):
        field = couple([par_codes[q, i] for i in range(8)], lambda i: par_coupling[q, i])
        spread = dot_nt(field.astype(BF16), transfer[pl.ds(4 * q, 4)].reshape(256, 64))
        for m in range(2):
            downs = []
            for c in (2 * m, 2 * m + 1):
                leaf = 4 * q + c
                codes = [leaf_codes[i, leaf] for i in range(8)]
                local = couple(codes, lambda i: coupling[leaf, i])
                downs.append(local + spread[:, 64 * c : 64 * (c + 1)])
            here = pl.ds(pl.multiple_of((2 * q + m) * 128, 128), 128)
            out[:, here] = side_by_side(*downs).astype(BF16)
        return carry

    lax.fori_loop(0, PARENTS, body, 0, unroll=True)


def far_down(leaf_codes, par_codes, gathered, coupling, par_coupling, transfer):
    smem = pl.BlockSpec(memory_space=pltpu.SMEM)
    vmem = pl.BlockSpec(memory_space=pltpu.VMEM)
    gathered = [pltpu.with_memory_space_constraint(part, pltpu.VMEM) for part in gathered]
    return pl.pallas_call(
        far_kernel,
        out_shape=jax.ShapeDtypeStruct((32, 2048), BF16),
        in_specs=[smem] * 2 + [vmem] * (len(gathered) + 3),
        out_specs=vmem,
        scratch_shapes=[pltpu.VMEM((32 * ROWS, 128), BF16)],
        cost_estimate=cost(FAR_US),
        compiler_params=pltpu.CompilerParams(vmem_limit_bytes=22 << 20),
    )(leaf_codes, par_codes, *gathered, coupling, par_coupling, transfer)


def sum_kernel(down, basis, keep, taken, passed, out):
    for m in range(LEAVES // 2):
        weights = diagonal(basis[2 * m], basis[2 * m + 1])
        pair = down[:, 128 * m : 128 * (m + 1)]
        result = jnp.dot(pair, weights, preferred_element_type=F32)
        here = slice(256 * m, 256 * (m + 1))
        near = keep[:, here].astype(F32) + taken[:32, here].astype(F32)
        out[:, here] = (result + (near + passed[:, here].astype(F32))).astype(BF16)


def far_and_sum(down, basis, *nears):
    vmem = pl.BlockSpec(memory_space=pltpu.VMEM)
    return pl.pallas_call(
        sum_kernel,
        out_shape=jax.ShapeDtypeStruct((32, 4096), BF16),
        in_specs=[vmem] * 5,
        out_specs=vmem,
        compiler_params=pltpu.CompilerParams(vmem_limit_bytes=8 << 20),
    )(down, basis, *nears)


def place(y, x, core):
    return (y % SIDE) * 8 + (x % SIDE) * 2 + core


def around(distance, first):
    pairs = []
    for y in range(SIDE):
        for x in range(SIDE):
            for core in range(2):
                alongx = (core == 0) == first
                to = place(y, x + distance, core) if alongx else place(y + distance, x, core)
                pairs.append((place(y, x, core), to))
    return pairs


def partners(first):
    return [
        (c * 4 + z, c * 4 + (z ^ (1 if (c % 2 == 0) == first else 3)))
        for c in range(32)
        for z in range(4)
    ]


OUTWARD = [(i, (i + (1 if i % 2 else -1)) % 32) for i in range(32)]
SWAP = [(i, i ^ 1) for i in range(32)]


def send(value, pairs, name):
    with jax.named_scope(name):
        return lax.ppermute(value, "clus", pairs)


def trade(value, first, name):
    with jax.named_scope(name):
        return lax.ppermute(value, ("clus", "rhs"), partners(first))


def per_device(
    sources,
    leaf_basis,
    transfer,
    far_leaf,
    leaf_coupling,
    far_par,
    par_coupling,
    near_list,
    near_count,
    near_block,
):
    clus, rhs = lax.axis_index("clus"), lax.axis_index("rhs")
    meta = jnp.stack([rhs, clus]).astype(jnp.int32)
    basis = jnp.swapaxes(leaf_basis, 1, 2)
    half = lax.dynamic_slice_in_dim(sources, (rhs & 1) * 64, 64, 0)
    far_mine = send(half, OUTWARD, "halo")
    sibling = send(sources, SWAP, "sibling")
    chunk, leaf_codes, par_codes, near_codes, sources_here, near_here = coefficients(
        meta,
        sources,
        basis,
        transfer,
        far_leaf.T,
        far_par,
        near_list.T,
        near_count.reshape(1, -1),
        near_block,
    )

    across = send(chunk, around(2, True), "across")
    before = send(chunk, around(1, True), "before")
    after = send(chunk, around(-1, True), "after")
    far_other = trade(far_mine, True, "halo_half")
    own = stacked(chunk, before, after, across, us=STACK_US)
    side_b = send(own, around(1, False), "side_b")
    side_a = send(own, around(-1, False), "side_a")
    keep, pass_on, give = near_partials(
        meta, near_codes, sources_here, sibling, far_mine, far_other, near_here
    )
    taken = trade(give, True, "near_pairs")
    own_other = send(own, SWAP, "swap_own")
    side_b, side_a, pass_on, own_other = lax.optimization_barrier(
        (side_b, side_a, pass_on, own_other)
    )
    half = own.shape[0] // 2
    far_b = send(side_b[:half], around(1, False), "far_b")
    far_a = send(side_a[half:], around(-1, False), "far_a")
    pass_on = added(pass_on, taken)
    passed = trade(pass_on, False, "near_last")
    far_b, far_a, pass_on = lax.optimization_barrier((far_b, far_a, pass_on))
    def swapped(name, *parts, step):
        pieces = [part[k : k + step] for part in parts for k in range(0, part.shape[0], step)]
        return tuple(send(piece, SWAP, name) for piece in pieces)

    mine = (own, side_b, side_a, far_b, far_a)
    inner = (own_other,) + swapped("swap_side", side_b, side_a, step=SIDE_STEP)
    outer = swapped("swap_far", far_b, far_a, step=FAR_STEP)
    gathered = mine + inner + outer
    down = far_down(leaf_codes, par_codes, gathered, leaf_coupling, par_coupling, transfer)
    return far_and_sum(down, basis, keep, taken, passed)


def solution(mesh):
    in_specs = (
        P(None, "clus"),
        P("clus", None, None),
        P("clus", None, None),
        P("clus", None),
        P("clus", None, None, None),
        P("clus", None),
        P("clus", None, None, None),
        P("clus", "rhs"),
        P("clus"),
        P("clus", "rhs", None, None),
    )
    return jax.shard_map(
        per_device, mesh=mesh, in_specs=in_specs, out_specs=P("rhs", "clus"), check_vma=False
    )
```
